32 devices in a mesh: dp: 8 (over y, x, core), seq: 4 (over z).
Axes of the slice: x: 2, y: 2, z: 4, core: 2. Of those that a mesh axis runs over, the one named last changes fastest.
Arguments:
- section_input: bfloat16 [8, 512, 768], P('dp', 'seq'), may hold values from -6 to 6
- conv_kernel: bfloat16 [5, 768, 768], P(None, None, 'seq'), may hold values from -0.09375 to 0.09375
- qkv_weight: bfloat16 [1536, 4608], P(None, 'seq'), may hold values from -0.15625 to 0.15625
- gain_in: float32 [768], replicated, may hold values from 0.1 to 1.9
- gain_mid: float32 [1536], replicated, may hold values from 0.1 to 1.9
- qkv_cotangent: bfloat16 [8, 256, 4608], P('dp', None, 'seq'), may hold values from -6 to 6
Outputs:
- qkv: bfloat16 [8, 256, 4608], P('dp', None, 'seq')
- input_grad: bfloat16 [8, 512, 768], P('dp', 'seq')
- kernel_grad: bfloat16 [5, 768, 768], P(None, None, 'seq')
- gain_in_grad: float32 [768], replicated
- gain_mid_grad: float32 [1536], replicated
- weight_grad: bfloat16 [1536, 4608], P(None, 'seq')
The draws below stay inside these ranges and needn't reach their ends.
All inputs are finite; a program needn't handle non-finite values.
Results may differ from the reference program's by a relative error of at most 0.02.
Values may be sent and summed in bfloat16 or wider, within the bound.
No kernel may reach another device: no remote copies, remote signals or barrier semaphores. Data moves between devices by JAX's collectives and lax.ppermute only.
A program may use at most 64 MiB of HBM per device.

```python
import math
import jax
import jax.numpy as jnp
from jax import lax

C = 768
D = 1536
TOKENS = 256
BATCH = 8
N_SEQ = 4


def spiked(result, own_key, source, target, blocks, factor):
    owner, partner = [(jnp.arange(result.shape[position]) // (result.shape[position] // blocks)).reshape([-1 if axis == position else 1 for axis in range(result.ndim)]) for position in (source, target)]
    chosen = jax.random.permutation(own_key, blocks)[partner]
    strong = (owner == chosen) | (owner == (partner + blocks // 2) % blocks)
    return jnp.where(strong, factor * result, result)


def block_levels(rng, shape, shards, least, high):
    loudness = 1.0
    for dim, shards_of in shards:
        draws = jax.random.uniform(jax.random.fold_in(jax.random.fold_in(rng, 6), dim), (shards_of,), jnp.float32, least / len(shards), high / len(shards))
        loudness = loudness * jnp.repeat(jnp.exp(draws), shape[dim] // shards_of).reshape((-1,) + (1,) * (len(shape) - 1 - dim))
    return loudness


def normal_values(key, shape, scale, most, split=(), dtype=jnp.bfloat16):
    result = scale * jax.random.normal(key, shape, jnp.float32)
    if split:
        result = result * block_levels(key, shape, split, -0.22, 0.18)
    return jnp.clip(result, -most, most).astype(dtype)


def heavy_noise(stream_key, dims, deviation, reach, split, heavy, kind=jnp.bfloat16):
    drawn = deviation * jax.random.normal(stream_key, dims, jnp.float32)
    if split:
        drawn = drawn * block_levels(stream_key, dims, split, -0.22, 0.18)
    return jnp.clip(spiked(drawn, jax.random.fold_in(stream_key, 3), *heavy), -reach, reach).astype(kind)


def setup_inputs(seed: int = 0) -> dict:
    keys = jax.random.split(jax.random.key(seed), 7)
    return {
        "section_input": normal_values(keys[0], (BATCH, 2 * TOKENS, C), 1.0, 6.0, ((0, 8), (1, 4))),
        "conv_kernel": normal_values(keys[1], (5, C, C), (5 * C) ** -0.5, 0.09375, ((2, 4),)),
        "qkv_weight": normal_values(keys[2], (D, 3 * D), D ** -0.5, 0.15625, ((1, 4),)),
        "gain_in": jnp.clip(1.0 + 0.18 * jax.random.normal(keys[3], (C,), jnp.float32), 0.1, 1.9),
        "gain_mid": jnp.clip(1.0 + 0.18 * jax.random.normal(keys[4], (D,), jnp.float32), 0.1, 1.9),
        "qkv_cotangent": heavy_noise(keys[5], (BATCH, TOKENS, 3 * D), 1.0, 6.0, ((0, 8), (2, 4)), (2, 1, 4, 2.0)),
    }


EPS = 1e-06

def inverse_rms(values):
    return lax.rsqrt(lax.optimization_barrier(jnp.mean(values * values, axis=-1, keepdims=True)) + EPS)

def one_sequence(section_row, conv_kernel, qkv_weight, gain_in, gain_mid, cotangent_row):
    length, chans = section_row.shape
    width = 2 * chans
    half = length // 2
    cols = qkv_weight.shape[1] // N_SEQ
    xfull = section_row.astype(jnp.float32)
    rone = inverse_rms(xfull)
    aone = xfull * rone
    normed_in = (aone * gain_in).astype(jnp.bfloat16)
    padded = jnp.pad(normed_in, ((2, 2), (0, 0)))
    conv_out = jnp.zeros((length, chans), jnp.float32)
    for k in range(5):
        conv_out = conv_out + jnp.dot(padded[k:k + length], conv_kernel[k], preferred_element_type=jnp.float32)
    sig = jax.nn.sigmoid(conv_out)
    section_out = xfull + conv_out * sig
    pooled = section_out.reshape(half, width)
    rtwo = inverse_rms(pooled)
    atwo = pooled * rtwo
    normed_mid = (atwo * gain_mid).astype(jnp.bfloat16)
    qkv = jnp.dot(normed_mid, qkv_weight, preferred_element_type=jnp.float32).astype(jnp.bfloat16)
    cot = cotangent_row.astype(jnp.float32)
    parts = jnp.einsum('tsc,dsc->tsd', cot.reshape(half, N_SEQ, cols), qkv_weight.astype(jnp.float32).reshape(width, N_SEQ, cols))
    parts = lax.optimization_barrier(parts.astype(jnp.bfloat16)).astype(jnp.float32)
    mid_grad = lax.optimization_barrier(jnp.sum(parts, axis=1))
    weight_term = lax.dot_general(normed_mid, cotangent_row, (((0,), (0,)), ((), ())), preferred_element_type=jnp.float32)
    gain_mid_term = lax.optimization_barrier(jnp.sum(mid_grad * atwo, axis=0))
    gmid = gain_mid * mid_grad
    pooled_grad = rtwo * (gmid - atwo * lax.optimization_barrier(jnp.mean(gmid * atwo, axis=-1, keepdims=True)))
    section_grad = pooled_grad.reshape(length, chans)
    conv_grad = (section_grad * sig * (1.0 + conv_out * (1.0 - sig))).astype(jnp.bfloat16)
    kernel_term = jnp.stack([lax.dot_general(padded[k:k + length], conv_grad, (((0,), (0,)), ((), ())), preferred_element_type=jnp.float32) for k in range(5)])
    grad_pad = jnp.pad(conv_grad, ((2, 2), (0, 0)))
    normed_grad = jnp.zeros((length, chans), jnp.float32)
    for k in range(5):
        normed_grad = normed_grad + lax.dot_general(grad_pad[4 - k:4 - k + length], conv_kernel[k], (((1,), (1,)), ((), ())), preferred_element_type=jnp.float32)
    gain_in_term = lax.optimization_barrier(jnp.sum(normed_grad * aone, axis=0))
    hin = gain_in * normed_grad
    input_grad = (section_grad + rone * (hin - aone * lax.optimization_barrier(jnp.mean(hin * aone, axis=-1, keepdims=True)))).astype(jnp.bfloat16)
    return (qkv, input_grad, kernel_term, gain_in_term, gain_mid_term, weight_term)

def reference(section_input, conv_kernel, qkv_weight, gain_in, gain_mid, qkv_cotangent):
    chans = section_input.shape[2]
    width = 2 * chans

    def step(carry, pair):
        outputs = one_sequence(pair[0], conv_kernel, qkv_weight, gain_in, gain_mid, pair[1])
        carry = (carry[0] + outputs[2], carry[1] + outputs[3], carry[2] + outputs[4], carry[3] + outputs[5])
        return (carry, (outputs[0], outputs[1]))
    start = (jnp.zeros((5, chans, chans), jnp.float32), jnp.zeros((chans,), jnp.float32), jnp.zeros((width,), jnp.float32), jnp.zeros(qkv_weight.shape, jnp.float32))
    totals, stacked = lax.scan(step, start, (section_input, qkv_cotangent))
    scale = 1.0 / math.sqrt(BATCH * TOKENS)
    return (stacked[0], stacked[1], (totals[0] * scale).astype(jnp.bfloat16), totals[1] * scale, totals[2] * scale, (totals[3] * scale).astype(jnp.bfloat16))
```

```python
import functools
import math

import jax
import jax.numpy as jnp
from jax import lax
from jax.experimental import pallas as pl
from jax.experimental.pallas import tpu as pltpu
from jax.sharding import PartitionSpec as P

EPS = 1e-06
F32 = jnp.float32
BF16 = jnp.bfloat16
VMEM = pl.BlockSpec(memory_space=pltpu.VMEM)
SMEM = pl.BlockSpec(memory_space=pltpu.SMEM)


def call(kernel, outs, args, scratch=(), flops=0, name=None):
    specs = [SMEM if a.dtype == jnp.int32 else VMEM for a in args]
    size = lambda a: a.size * a.dtype.itemsize
    moved = sum(map(size, args)) + sum(map(size, outs))
    return pl.pallas_call(
        kernel,
        out_shape=tuple(outs),
        in_specs=specs,
        out_specs=tuple(VMEM for _ in outs),
        scratch_shapes=list(scratch),
        compiler_params=pltpu.CompilerParams(vmem_limit_bytes=56 << 20),
        cost_estimate=pl.CostEstimate(flops=flops, bytes_accessed=moved, transcendentals=0),
        name=name,
    )(*args)


def shaped(shape, dtype):
    return jax.ShapeDtypeStruct(shape, dtype)


def dot(a, b):
    return jnp.dot(a, b, preferred_element_type=F32)


def dot_nt(a, b):
    return lax.dot_general(a, b, (((1,), (1,)), ((), ())), preferred_element_type=F32)


def dot_tn(a, b):
    return lax.dot_general(a, b, (((0,), (0,)), ((), ())), preferred_element_type=F32)


def later(v):
    row = lax.broadcasted_iota(jnp.int32, v.shape, 0)
    return jnp.where(row == 0, 0.0, pltpu.roll(v, 1, 0))


def sooner(v):
    rows = v.shape[0]
    row = lax.broadcasted_iota(jnp.int32, v.shape, 0)
    return jnp.where(row == rows - 1, 0.0, pltpu.roll(v, rows - 1, 0))


def inv_rms(v):
    return lax.rsqrt(jnp.mean(v * v, axis=-1, keepdims=True) + EPS)


def mid_kernel(n, c, chans, cot, w, out):
    g = cot[...]
    for b in range(n):
        cols = jnp.concatenate(
            [w[b * c : (b + 1) * c, :], w[chans + b * c : chans + (b + 1) * c, :]], axis=0
        )
        out[b] = dot_nt(g, cols).astype(BF16)


def conv_kernel_fwd(n, c, chans, *refs):
    me = refs[0][0]
    blocks = refs[1 : 1 + n]
    taps, gain, pooled_msg, pooled, conv_out, nin, xs = refs[1 + n :]
    rows = blocks[0].shape[0]
    gains = gain[...]
    for k in range(n):
        at = pl.multiple_of(lax.rem(me - k + n, n) * rows, rows)
        v = blocks[k][...]
        xs[pl.ds(at, rows), :] = v
        for h in range(2):
            f = v[:, h * chans : (h + 1) * chans].astype(F32)
            nin[pl.ds(at, rows), h * chans : (h + 1) * chans] = (f * inv_rms(f) * gains).astype(BF16)
    xe, xo = nin[:, :chans], nin[:, chans:]
    k0, k1, k2, k3, k4 = (taps[k] for k in range(5))
    even = dot(xe, k2) + dot(xo, k3) + later(dot(xe, k0) + dot(xo, k1)) + sooner(dot(xe, k4))
    odd = dot(xe, k1) + dot(xo, k2) + later(dot(xo, k0)) + sooner(dot(xe, k3) + dot(xo, k4))
    conv = jnp.concatenate([even, odd], axis=1)
    row = lax.broadcasted_iota(jnp.int32, (chans, c), 0)
    col = lax.broadcasted_iota(jnp.int32, (chans, c), 1)
    pick = jnp.where(row == col + me * c, 1.0, 0.0).astype(BF16)
    own = jnp.concatenate([dot(xs[:, :chans], pick), dot(xs[:, chans:], pick)], axis=1)
    total = own + conv * jax.nn.sigmoid(conv)
    conv_out[...] = conv
    pooled[...] = total
    pooled_msg[...] = total.astype(BF16)


def norm_kernel(n, c, chans, *refs):
    me = refs[0][0]
    blocks = refs[1 : 1 + n]
    gains, nmt, rtwo = refs[1 + n :]
    squares = 0.0
    for k in range(n):
        v = blocks[k][...].astype(F32)
        squares = squares + jnp.sum(v * v, axis=1, keepdims=True)
    r = lax.rsqrt(squares * (1.0 / (2 * chans)) + EPS)
    rtwo[...] = r
    for k in range(n):
        b = lax.rem(me - k + n, n)
        v = blocks[k][...].astype(F32) * r * gains[pl.ds(b, 1), :]
        t = v.T.astype(BF16)
        for h in range(2):
            at = pl.multiple_of(h * chans + b * c, c & -c)
            nmt[pl.ds(at, c), :] = t[h * c : (h + 1) * c, :]


def qkv_kernel(nmt, w, cot, qkv, part):
    q = dot_tn(nmt[...], w[...])
    qkv[...] = q.astype(BF16)
    row = jnp.sum(q * cot[...].astype(F32), axis=1, keepdims=True)
    part[...] = jnp.broadcast_to(row, (row.shape[0], 128)).T[:8, :]


def weight_kernel(m, scale, *refs):
    me = refs[0][0]
    nms = refs[1]
    cots = refs[2 : 2 + m]
    out = refs[2 + m]
    total = dot(nms[me], cots[0][...])
    for k in range(1, m):
        total = total + dot(nms[me ^ k], cots[k][...])
    out[...] = (total * scale).astype(BF16)


def back_kernel(n, c, chans, m, *refs):
    seq_at, dp_at = refs[0][0], refs[0][1]
    parts = refs[1 : 1 + n]
    (mids, pooled, rtwo, conv_out, gmid, gin, nin, taps, keep, send, msg, sums, kg) = refs[1 + n :]
    width = 2 * chans
    mid = mids[0].astype(F32)
    for b in range(1, n):
        mid = mid + mids[b].astype(F32)
    r = rtwo[...]
    atwo = pooled[...] * r
    rowsum = parts[0][...]
    for k in range(1, n):
        rowsum = rowsum + parts[k][...]
    half = atwo.shape[0]
    mean = jnp.concatenate([rowsum] * 16, axis=0).T[:, :1] * (1.0 / width)
    mid_sum = jnp.sum(mid * atwo, axis=0, keepdims=True)
    section = r * (gmid[pl.ds(seq_at, 1), :] * mid - atwo * mean)
    conv = conv_out[...]
    sig = jax.nn.sigmoid(conv)
    cg = section * sig * (1.0 + conv * (1.0 - sig))
    cg = cg.astype(BF16).astype(F32)
    ge, go = cg[:, :c], cg[:, c:]
    bf = lambda v: v.astype(BF16)
    g0, gp, gm = bf(ge), bf(sooner(ge)), bf(later(ge))
    o0, op, om = bf(go), bf(sooner(go)), bf(later(go))
    es, os_ = (gp, o0, g0, om, gm), (op, gp, o0, g0, om)
    xe, xo = nin[:, :chans], nin[:, chans:]
    kg[...] = dot_tn(xe, jnp.concatenate(es, axis=1)) + dot_tn(xo, jnp.concatenate(os_, axis=1))
    rows = chans // m
    core = lax.rem(dp_at, 2)
    for q in range(m // 2):
        keep[q] = kg[pl.ds(pl.multiple_of((2 * q + core) * rows, rows & -rows), rows), :]
        send[q] = kg[pl.ds(pl.multiple_of((2 * q + 1 - core) * rows, rows & -rows), rows), :].astype(BF16)
    gains = gin[...]
    acc = 0.0
    block = half // n
    for h, terms in ((0, es), (1, os_)):
        ng = dot_nt(terms[0], taps[0])
        for k in range(1, 5):
            ng = ng + dot_nt(terms[k], taps[k])
        acc = acc + jnp.sum(ng * (nin[:, h * chans : (h + 1) * chans].astype(F32)), axis=0, keepdims=True)
        for b in range(n):
            msg[b, :, h * chans : (h + 1) * chans] = ng[b * block : (b + 1) * block, :].astype(BF16)
    line = lax.broadcasted_iota(jnp.int32, sums.shape, 0)
    wide = jnp.concatenate([mid_sum, jnp.zeros((1, chans - 2 * c), F32)], axis=1)
    sums[...] = jnp.where(line == 0, acc / gains, jnp.where(line == 1 + seq_at, wide, 0.0))
    for b in range(n):
        msg[b, :, width:] = section[b * block : (b + 1) * block, :].astype(BF16)


def split_kernel(q, at, keep, recv, *outs):
    me = at[1] // 2
    for k in range(q):
        v = keep[me ^ k] + recv[me ^ k].astype(F32)
        outs[k][...] = v.astype(outs[k].dtype)


def finish_kernel(scale, *refs):
    total = refs[0][...]
    for r in refs[1:-1]:
        total = total + r[...].astype(F32)
    refs[-1][...] = (total * scale).astype(BF16)


def place_taps_kernel(m, c, *refs):
    me = refs[0][1]
    shares = refs[1 : 1 + m]
    out = refs[1 + m]
    rows = shares[0].shape[0]
    for k in range(m):
        at = pl.multiple_of((me ^ k) * rows, rows & -rows)
        v = shares[k][...]
        for t in range(5):
            out[t, pl.ds(at, rows), :] = v[:, t * c : (t + 1) * c].astype(out.dtype)


def place_rows_kernel(m, *refs):
    me = refs[0][1]
    shares = refs[1 : 1 + m]
    out = refs[1 + m]
    rows = shares[0].shape[0]
    for k in range(m):
        at = pl.multiple_of((me ^ k) * rows, rows & -rows)
        out[pl.ds(at, rows), :] = shares[k][...]


def input_kernel(n, c, chans, got, own, gin, out):
    total = got[0, :, : 2 * chans].astype(F32)
    for b in range(1, n):
        total = total + got[b, :, : 2 * chans].astype(F32)
    gains = gin[...]
    for h in range(2):
        x = own[:, h * chans : (h + 1) * chans].astype(F32)
        r = inv_rms(x)
        a = x * r
        g = gains * total[:, h * chans : (h + 1) * chans]
        sect = jnp.concatenate(
            [got[b, :, 2 * chans + h * c : 2 * chans + (h + 1) * c] for b in range(n)], axis=1
        ).astype(F32)
        v = sect + r * (g - a * jnp.mean(g * a, axis=-1, keepdims=True))
        out[:, h * chans : (h + 1) * chans] = v.astype(BF16)


def body(section_input, conv_kernel, qkv_weight, gain_in, gain_mid, qkv_cotangent):
    x = section_input[0]
    cot = qkv_cotangent[0]
    length, chans = x.shape
    c = conv_kernel.shape[2]
    width, cols = qkv_weight.shape
    n, m = lax.axis_size("seq"), lax.axis_size("dp")
    half = length // 2 * n
    scale = 1.0 / math.sqrt(m * half)
    seq_at, dp_at = lax.axis_index("seq"), lax.axis_index("dp")
    at = jnp.stack([seq_at, dp_at]).astype(jnp.int32)
    from_ring = lambda v: [v] + [
        lax.ppermute(v, "seq", [(i, (i + k) % n) for i in range(n)]) for k in range(1, n)
    ]
    across = lambda v, k: lax.ppermute(v, "dp", [(i, i ^ k) for i in range(m)])

    def to_all(v):
        firsts = [v] + [across(v, k) for k in range(2, m, 2)]
        both = []
        for f in firsts:
            both += [f, across(f, 1)]
        return both

    own = x.reshape(length // 2, 2 * chans)
    xs = from_ring(own)
    gin = gain_in.reshape(1, chans)
    gmid = gain_mid.reshape(2, n, c).transpose(1, 0, 2).reshape(n, 2 * c)
    cots = to_all(cot)
    (mid_msg,) = call(
        functools.partial(mid_kernel, n, c, chans),
        [shaped((n, half, 2 * c), BF16)],
        [cot, qkv_weight],
        flops=2 * half * width * cols,
        name="mid_parts",
    )
    pooled_msg, pooled, conv_out, nin = call(
        functools.partial(conv_kernel_fwd, n, c, chans),
        [
            shaped((half, 2 * c), BF16),
            shaped((half, 2 * c), F32),
            shaped((half, 2 * c), F32),
            shaped((half, width), BF16),
        ],
        [at, *xs, conv_kernel, gin],
        scratch=[pltpu.VMEM((half, width), BF16)],
        flops=20 * half * chans * c,
        name="conv_forward",
    )
    blocks = from_ring(pooled_msg)
    nmt, rtwo = call(
        functools.partial(norm_kernel, n, c, chans),
        [shaped((width, half), BF16), shaped((half, 1), F32)],
        [at, *blocks, gmid],
        name="norm_mid",
    )
    mids = lax.all_to_all(mid_msg, "seq", 0, 0, tiled=True)
    nms = lax.all_to_all(nmt.reshape(m, width // m, half), "dp", 0, 0, tiled=True)
    qkv, part = call(
        qkv_kernel,
        [shaped((half, cols), BF16), shaped((8, half), F32)],
        [nmt, qkv_weight, cot],
        flops=2 * half * width * cols,
        name="qkv",
    )
    parts = from_ring(part)
    (wshare,) = call(
        functools.partial(weight_kernel, m, scale),
        [shaped((width // m, cols), BF16)],
        [at[1:], nms, *cots],
        flops=2 * half * width * cols,
        name="weight_share",
    )
    wshares = to_all(wshare)
    rows = chans // m
    keep, send, msg, sums = call(
        functools.partial(back_kernel, n, c, chans, m),
        [
            shaped((m // 2, rows, 5 * c), F32),
            shaped((m // 2, rows, 5 * c), BF16),
            shaped((n, half // n, width + 2 * c), BF16),
            shaped((-(-(1 + n) // 8) * 8, chans), F32),
        ],
        [at, *parts, mids, pooled, rtwo, conv_out, gmid, gin, nin, conv_kernel],
        scratch=[pltpu.VMEM((chans, 5 * c), F32)],
        flops=40 * half * chans * c,
        name="conv_backward",
    )
    got = lax.all_to_all(msg, "seq", 0, 0, tiled=True)
    split = call(
        functools.partial(split_kernel, m // 2),
        [shaped((rows, 5 * c), F32)] + [shaped((rows, 5 * c), BF16)] * (m // 2 - 1),
        [at, keep, across(send, 1)],
        name="core_sum",
    )
    (kshare,) = call(
        functools.partial(finish_kernel, scale),
        [shaped((rows, 5 * c), BF16)],
        [split[0]] + [across(split[k], 2 * k) for k in range(1, m // 2)],
        name="chip_sum",
    )
    kshares = to_all(kshare)
    k = 1
    while k < m:
        sums = sums + across(sums, k)
        k *= 2
    totals = from_ring(sums)
    total = totals[0]
    for v in totals[1:]:
        total = total + v
    total = total * scale
    (input_grad,) = call(
        functools.partial(input_kernel, n, c, chans),
        [shaped((length // 2, 2 * chans), BF16)],
        [got, own, gin],
        name="input_grad",
    )
    (kernel_grad,) = call(
        functools.partial(place_taps_kernel, m, c),
        [shaped((5, chans, c), BF16 if rows % 16 == 0 else F32)],
        [at, *kshares],
        name="place_kernel_grad",
    )
    (weight_grad,) = call(
        functools.partial(place_rows_kernel, m),
        [shaped((width, cols), BF16)],
        [at, *wshares],
        name="place_weight_grad",
    )
    gain_mid_grad = total[1 : 1 + n, : 2 * c].reshape(n, 2, c).transpose(1, 0, 2).reshape(width)
    return (
        qkv[None],
        input_grad.reshape(1, length, chans),
        kernel_grad.astype(BF16),
        total[0],
        gain_mid_grad,
        weight_grad,
    )


def solution(mesh):
    placed = (
        P("dp", "seq", None),
        P(None, None, "seq"),
        P(None, "seq"),
        P(),
        P(),
        P("dp", None, "seq"),
    )
    return jax.shard_map(
        body,
        mesh=mesh,
        in_specs=placed,
        out_specs=(
            P("dp", None, "seq"),
            P("dp", "seq", None),
            P(None, None, "seq"),
            P(),
            P(),
            P(None, "seq"),
        ),
        check_vma=False,
    )
```

```python
import functools
import math

import jax
import jax.numpy as jnp
from jax import lax
from jax.experimental import pallas as pl
from jax.experimental.pallas import tpu as pltpu
from jax.sharding import PartitionSpec as P

EPS = 1e-06
SPARE = 12
F32 = jnp.float32
BF16 = jnp.bfloat16
VMEM = pl.BlockSpec(memory_space=pltpu.VMEM)
ANY = pl.BlockSpec(memory_space=pl.ANY)


def call(kernel, outs, args, held=(), scratch=(), name=None):
    lanes = lambda v: math.prod(v.shape[:-1]) * -(-v.shape[-1] // 128) * 128 * v.dtype.itemsize
    need = sum(map(lanes, [*args, *outs, *scratch]))
    return pl.pallas_call(
        kernel,
        out_shape=tuple(outs) + tuple(shaped(v.shape, v.dtype) for v in held),
        in_specs=[VMEM] * len(args) + [ANY] * len(held),
        out_specs=tuple([VMEM] * len(outs) + [ANY] * len(held)),
        input_output_aliases={len(args) + i: len(outs) + i for i in range(len(held))},
        scratch_shapes=list(scratch),
        compiler_params=pltpu.CompilerParams(vmem_limit_bytes=min(56 << 20, need + (SPARE << 20))),
        cost_estimate=pl.CostEstimate(flops=0, bytes_accessed=0, transcendentals=0),
        name=name,
    )(*args, *held)


def shaped(shape, dtype):
    return jax.ShapeDtypeStruct(shape, dtype)


def dot(a, b):
    return jnp.dot(a, b, preferred_element_type=F32)


def dot_nt(a, b):
    return lax.dot_general(a, b, (((1,), (1,)), ((), ())), preferred_element_type=F32)


def dot_tn(a, b):
    return lax.dot_general(a, b, (((0,), (0,)), ((), ())), preferred_element_type=F32)


def later(v):
    row = lax.broadcasted_iota(jnp.int32, v.shape, 0)
    return jnp.where(row == 0, 0.0, pltpu.roll(v, 1, 0))


def sooner(v):
    rows = v.shape[0]
    row = lax.broadcasted_iota(jnp.int32, v.shape, 0)
    return jnp.where(row == rows - 1, 0.0, pltpu.roll(v, rows - 1, 0))


def inv_rms(v):
    return lax.rsqrt(jnp.mean(v * v, axis=-1, keepdims=True) + EPS)


def mid_kernel(n, c, chans, cot, w, *refs):
    outs = refs[1 : 1 + n]
    me = lax.axis_index("seq")
    g = cot[...]
    for k in range(n):
        at = pl.multiple_of(lax.rem(me + k, n) * c, c & -c)
        rows = jnp.concatenate([w[pl.ds(at, c), :], w[pl.ds(chans + at, c), :]], axis=0)
        outs[k][...] = dot_nt(g, rows).astype(BF16)


def conv_fwd_kernel(n, c, chans, *refs):
    me = lax.axis_index("seq")
    blocks = refs[:n]
    taps, gain, pooled_msg, pooled, conv_out, nin, xs = refs[n:]
    rows = blocks[0].shape[0]
    gains = gain[...]
    for k in range(n):
        at = pl.multiple_of(lax.rem(me - k + n, n) * rows, rows)
        v = blocks[k][...]
        xs[pl.ds(at, rows), :] = v
        for h in range(2):
            f = v[:, h * chans : (h + 1) * chans].astype(F32)
            nin[pl.ds(at, rows), h * chans : (h + 1) * chans] = (f * inv_rms(f) * gains).astype(BF16)
    xe, xo = nin[:, :chans], nin[:, chans:]
    k0, k1, k2, k3, k4 = (taps[k] for k in range(5))
    even = dot_nt(xe, k2) + dot_nt(xo, k3) + later(dot_nt(xe, k0) + dot_nt(xo, k1)) + sooner(dot_nt(xe, k4))
    odd = dot_nt(xe, k1) + dot_nt(xo, k2) + later(dot_nt(xo, k0)) + sooner(dot_nt(xe, k3) + dot_nt(xo, k4))
    conv = jnp.concatenate([even, odd], axis=1)
    row = lax.broadcasted_iota(jnp.int32, (chans, c), 0)
    col = lax.broadcasted_iota(jnp.int32, (chans, c), 1)
    pick = jnp.where(row == col + me * c, 1.0, 0.0).astype(BF16)
    own = jnp.concatenate([dot(xs[:, :chans], pick), dot(xs[:, chans:], pick)], axis=1)
    total = own + conv * jax.nn.sigmoid(conv)
    conv_out[...] = conv
    pooled[...] = total
    pooled_msg[...] = total.astype(BF16)


def norm_kernel(n, c, chans, *refs):
    me = lax.axis_index("seq")
    blocks = refs[:n]
    gains = refs[n]
    nmt, rtwo = refs[2 * n + 1 : 2 * n + 3]
    squares = 0.0
    for k in range(n):
        v = blocks[k][...].astype(F32)
        squares = squares + jnp.sum(v * v, axis=1, keepdims=True)
    r = lax.rsqrt(squares * (1.0 / (2 * chans)) + EPS)
    rtwo[...] = r
    for k in range(n):
        b = lax.rem(me - k + n, n)
        v = blocks[k][...].astype(F32) * r * gains[pl.ds(b, 1), :]
        t = v.T.astype(BF16)
        for h in range(2):
            at = pl.multiple_of(h * chans + b * c, c & -c)
            nmt[pl.ds(at, c), :] = t[h * c : (h + 1) * c, :]


def qkv_kernel(nmt, w, cot, qkv, part):
    q = dot_tn(nmt[...], w[...])
    qkv[...] = q.astype(BF16)
    row = jnp.sum(q * cot[...].astype(F32), axis=1, keepdims=True)
    part[...] = jnp.broadcast_to(row, (row.shape[0], 128)).T[:8, :]


def weight_kernel(m, scale, nms, cots, out):
    total = dot(nms[0], cots[0])
    for b in range(1, m):
        total = total + dot(nms[b], cots[b])
    out[...] = (total * scale).astype(BF16)


def back_kernel(n, c, chans, m, *refs):
    seq_at = lax.axis_index("seq")
    core = lax.rem(lax.axis_index("dp"), 2)
    parts, mids = refs[:n], refs[n : 2 * n]
    pooled, rtwo, conv_out, gmid, nin, keep, send, evens, odds, section_out, mid_sum = refs[2 * n :]
    mid = mids[0][...].astype(F32)
    for v in mids[1:]:
        mid = mid + v[...].astype(F32)
    r = rtwo[...]
    atwo = pooled[...] * r
    rowsum = parts[0][...]
    for v in parts[1:]:
        rowsum = rowsum + v[...]
    mean = jnp.concatenate([rowsum] * 16, axis=0).T[:, :1] * (1.0 / (2 * chans))
    mid_sum[...] = jnp.sum(mid * atwo, axis=0, keepdims=True)
    section = r * (gmid[pl.ds(seq_at, 1), :] * mid - atwo * mean)
    section_out[...] = section.astype(BF16)
    conv = conv_out[...]
    sig = jax.nn.sigmoid(conv)
    cg = section * sig * (1.0 + conv * (1.0 - sig))
    cg = cg.astype(BF16).astype(F32)
    ge, go = cg[:, :c], cg[:, c:]
    bf = lambda v: v.astype(BF16)
    g0, gp, gm = bf(ge), bf(sooner(ge)), bf(later(ge))
    o0, op, om = bf(go), bf(sooner(go)), bf(later(go))
    evens[...] = jnp.concatenate((gp, o0, g0, om, gm), axis=1)
    odds[...] = jnp.concatenate((op, gp, o0, g0, om), axis=1)
    wide, rows = chans // 2, 5 * c // (m // 2)
    for out, which in ((send, 1 - core), (keep, core)):
        at = pl.multiple_of(which * wide, wide & -wide)
        kg = dot_tn(evens[...], nin[:, pl.ds(at, wide)]) + dot_tn(odds[...], nin[:, pl.ds(chans + at, wide)])
        for q in range(m // 2):
            out[q] = kg[q * rows : (q + 1) * rows, :].astype(out.dtype)


def input_part_kernel(n, c, chans, evens, odds, section, mid_sum, gin, nin, taps, msg, sums):
    width = 2 * chans
    block = evens.shape[0] // n
    acc = 0.0
    for h, g in ((0, evens), (1, odds)):
        ng = dot(g[...], taps[...])
        acc = acc + jnp.sum(ng * nin[:, h * chans : (h + 1) * chans].astype(F32), axis=0, keepdims=True)
        for b in range(n):
            msg[b, :, h * chans : (h + 1) * chans] = ng[b * block : (b + 1) * block, :].astype(BF16)
    for b in range(n):
        msg[b, :, width:] = section[b * block : (b + 1) * block, :]
    acc = acc / gin[...]
    wide = chans // 2
    own = mid_sum[...]
    if 2 * c < wide:
        own = jnp.concatenate([own, jnp.zeros((1, wide - 2 * c), F32)], axis=1)
    line = lax.broadcasted_iota(jnp.int32, sums.shape, 0)
    pick = lambda i, v: jnp.where(line == i, v, 0.0)
    sums[...] = pick(0, acc[:, :wide]) + pick(1, acc[:, wide:]) + pick(2, own)


def split_kernel(q, *refs):
    keep, recv, outs = refs[0], refs[1], refs[-q:]
    me = lax.axis_index("dp") // 2
    for k in range(q):
        v = keep[me ^ k] + recv[me ^ k].astype(F32)
        outs[k][...] = v.astype(outs[k].dtype)


def in_two(v):
    high = v.astype(BF16).astype(F32)
    return jnp.concatenate([high, v - high], axis=0).astype(BF16)


def finish_kernel(n, q, scale, *refs):
    me = lax.axis_index("seq")
    shares, sums, out = refs[:q], refs[q : q + n], refs[q + n]
    total = shares[0][...]
    for r in shares[1:]:
        total = total + r[...].astype(F32)
    rows = total.shape[0]
    out[:rows, :] = (total * scale).astype(BF16)
    both = sums[0][...]
    for r in sums[1:]:
        both = both + r[...]
    line = lax.broadcasted_iota(jnp.int32, both.shape, 0)
    tail = jnp.where(line < 2, both, 0.0)
    for k in range(n):
        row = jnp.broadcast_to(sums[k][2:3, :], both.shape)
        tail = jnp.where(line == 2 + lax.rem(me - k + n, n), row, tail)
    out[rows:, :] = in_two(tail * scale)


def joined(tail):
    return tail[:8].astype(F32) + tail[8:].astype(F32)


def half_kernel(q, *refs):
    me = lax.axis_index("dp") // 2
    shares, out = refs[:q], refs[q]
    rows = shares[0].shape[0] - 16
    tail = 0.0
    for k in range(q):
        at = pl.multiple_of((me ^ k) * rows, rows & -rows)
        out[pl.ds(at, rows), :] = shares[k][:rows, :]
        tail = tail + joined(shares[k][rows:, :])
    out[q * rows :, :] = in_two(tail)


def place_kernel(n, c, mine, other, taps, gain_in, gain_mid):
    core = lax.rem(lax.axis_index("dp"), 2)
    rows, wide = taps.shape[0], mine.shape[1]
    for ref, which in ((mine, core), (other, 1 - core)):
        side = pl.multiple_of(which * wide, wide & -wide)
        taps[:, pl.ds(side, wide)] = ref[:rows, :]
    total = joined(mine[rows:, :]) + joined(other[rows:, :])
    gain_in[...] = total[:2, :]
    gain_mid[...] = total[2 : 2 + n, : 2 * c]


def input_kernel(n, c, chans, got, own, gin, out):
    total = got[0, :, : 2 * chans].astype(F32)
    for b in range(1, n):
        total = total + got[b, :, : 2 * chans].astype(F32)
    gains = gin[...]
    for h in range(2):
        x = own[:, h * chans : (h + 1) * chans].astype(F32)
        r = inv_rms(x)
        a = x * r
        g = gains * total[:, h * chans : (h + 1) * chans]
        sect = jnp.concatenate(
            [got[b, :, 2 * chans + h * c : 2 * chans + (h + 1) * c] for b in range(n)], axis=1
        ).astype(F32)
        v = sect + r * (g - a * jnp.mean(g * a, axis=-1, keepdims=True))
        out[:, h * chans : (h + 1) * chans] = v.astype(BF16)


def body(section_input, conv_kernel, qkv_weight, gain_in, gain_mid, qkv_cotangent):
    x = section_input[0]
    cot = qkv_cotangent[0]
    length, chans = x.shape
    c = conv_kernel.shape[2]
    width, cols = qkv_weight.shape
    n, m = lax.axis_size("seq"), lax.axis_size("dp")
    half = length // 2 * n
    scale = 1.0 / math.sqrt(m * half)
    shift = lambda v, k: lax.ppermute(v, "seq", [(i, (i + k) % n) for i in range(n)])
    from_ring = lambda v: [v] + [shift(v, k) for k in range(1, n)]
    across = lambda v, k: lax.ppermute(v, "dp", [(i, i ^ k) for i in range(m)])

    taps = conv_kernel.transpose(0, 2, 1)
    own = x.reshape(length // 2, width)
    xs = from_ring(own)
    gin = gain_in.reshape(1, chans)
    gmid = gain_mid.reshape(2, n, c).transpose(1, 0, 2).reshape(n, 2 * c)
    cots = lax.all_gather(cot, "dp", axis=0)
    pooled_msg, pooled, conv_out, nin = call(
        functools.partial(conv_fwd_kernel, n, c, chans),
        [
            shaped((half, 2 * c), BF16),
            shaped((half, 2 * c), F32),
            shaped((half, 2 * c), F32),
            shaped((half, width), BF16),
        ],
        [*xs, taps, gin],
        scratch=[pltpu.VMEM((half, width), BF16)],
        name="conv_forward",
    )
    blocks = from_ring(pooled_msg)
    *mid_msgs, pooled = call(
        functools.partial(mid_kernel, n, c, chans),
        [shaped((half, 2 * c), BF16)] * n,
        [cot, qkv_weight],
        held=[pooled],
        name="mid_parts",
    )
    nmt, rtwo, *mid_msgs = call(
        functools.partial(norm_kernel, n, c, chans),
        [shaped((width, half), BF16), shaped((half, 1), F32)],
        [*blocks, gmid],
        held=mid_msgs,
        name="norm_mid",
    )
    mids = [mid_msgs[0]] + [shift(mid_msgs[k], k) for k in range(1, n)]
    nms = lax.all_to_all(nmt.reshape(m, width // m, half), "dp", 0, 0, tiled=True)
    qkv, part = call(
        qkv_kernel,
        [shaped((half, cols), BF16), shaped((8, half), F32)],
        [nmt, qkv_weight, cot],
        name="qkv",
    )
    parts = from_ring(part)
    (wshare,) = call(
        functools.partial(weight_kernel, m, scale),
        [shaped((width // m, cols), BF16)],
        [nms, cots],
        name="weight_share",
    )
    weight_grad = lax.all_gather(wshare, "dp", axis=0, tiled=True)
    chips = m // 2
    rows, wide = 5 * c // chips, chans // 2
    keep, send, evens, odds, section, mid_sum = call(
        functools.partial(back_kernel, n, c, chans, m),
        [
            shaped((chips, rows, wide), F32),
            shaped((chips, rows, wide), BF16),
            shaped((half, 5 * c), BF16),
            shaped((half, 5 * c), BF16),
            shaped((half, 2 * c), BF16),
            shaped((1, 2 * c), F32),
        ],
        [*parts, *mids, pooled, rtwo, conv_out, gmid, nin],
        name="conv_backward",
    )
    msg, sums = call(
        functools.partial(input_part_kernel, n, c, chans),
        [shaped((n, half // n, width + 2 * c), BF16), shaped((8, wide), F32)],
        [evens, odds, section, mid_sum, gin, nin, taps.reshape(5 * c, chans)],
        name="input_part",
    )
    got = lax.all_to_all(msg, "seq", 0, 0, tiled=True)
    if rows % 16 == 0 and n <= 6:
        split = call(
            functools.partial(split_kernel, chips),
            [shaped((rows, wide), F32)] + [shaped((rows, wide), BF16)] * (chips - 1),
            [keep, across(send, 1)],
            name="core_sum",
        )
        (kshare,) = call(
            functools.partial(finish_kernel, n, chips, scale),
            [shaped((rows + 16, wide), BF16)],
            [split[0]] + [across(split[k], 2 * k) for k in range(1, chips)] + from_ring(sums),
            name="chip_sum",
        )
        (mine,) = call(
            functools.partial(half_kernel, chips),
            [shaped((5 * c + 16, wide), BF16)],
            [kshare] + [across(kshare, k) for k in range(2, m, 2)],
            name="kernel_grad_half",
        )
        taps_grad, gain_in_grad, gain_mid_grad = call(
            functools.partial(place_kernel, n, c),
            [shaped((5 * c, chans), BF16), shaped((2, wide), F32), shaped((n, 2 * c), F32)],
            [mine, across(mine, 1)],
            name="kernel_grad",
        )
    else:
        core = lax.axis_index("dp") % 2
        both = jnp.stack([keep, send.astype(F32)])
        both = jnp.where(core == 0, both, both[::-1]).transpose(1, 2, 0, 3).reshape(5 * c, chans)
        both, sums = lax.psum((both, sums), "dp")
        taps_grad, sums = (both * scale).astype(BF16), sums * scale
        sums = lax.all_gather(sums, "seq")
        gain_in_grad = jnp.sum(sums[:, :2], axis=0)
        gain_mid_grad = sums[:, 2, : 2 * c]
    (input_grad,) = call(
        functools.partial(input_kernel, n, c, chans),
        [shaped((length // 2, width), BF16)],
        [got, own, gin],
        name="input_grad",
    )
    return (
        qkv[None],
        input_grad.reshape(1, length, chans),
        taps_grad.reshape(5, c, chans).transpose(0, 2, 1),
        gain_in_grad.reshape(chans),
        gain_mid_grad.reshape(n, 2, c).transpose(1, 0, 2).reshape(width),
        weight_grad,
    )


def solution(mesh):
    placed = (
        P("dp", "seq", None),
        P(None, None, "seq"),
        P(None, "seq"),
        P(),
        P(),
        P("dp", None, "seq"),
    )
    return jax.shard_map(
        body,
        mesh=mesh,
        in_specs=placed,
        out_specs=(
            P("dp", None, "seq"),
            P("dp", "seq", None),
            P(None, None, "seq"),
            P(),
            P(),
            P(None, "seq"),
        ),
        check_vma=False,
    )
```

```python
import functools
import math

import jax
import jax.numpy as jnp
from jax import lax
from jax.experimental import pallas as pl
from jax.experimental.pallas import tpu as pltpu
from jax.sharding import PartitionSpec as P

EPS = 1e-06
WAIT = 4e10
SPARE = 12
F32 = jnp.float32
BF16 = jnp.bfloat16
ANY = pl.BlockSpec(memory_space=pl.ANY)
HBM = pl.BlockSpec(memory_space=pltpu.HBM)
VMEM = pl.BlockSpec(memory_space=pltpu.VMEM)


class In:
    def __init__(self, ref, copy=None):
        self.ref, self.copy = ref, copy
        if copy is not None:
            copy.start()

    def __call__(self):
        if self.copy is not None:
            self.copy.wait()
            self.copy = None
        return self.ref


def shaped(shape, dtype):
    return jax.ShapeDtypeStruct(shape, dtype)


class Far:
    def __init__(self, value):
        self.value = value


def call(kernel, args, outs=(), free=(), kept=(), after=(), near=(), spill=(), scratch=(), flops=0, name=None):
    within = lambda v: pltpu.with_memory_space_constraint(v, pltpu.VMEM)
    near, spill = [within(v) for v in near], [within(v) for v in spill]
    far = [i for i, v in enumerate(args) if isinstance(v, Far)]
    args = [pltpu.with_memory_space_constraint(v.value, pltpu.HBM) if isinstance(v, Far) else v for v in args]
    count, skip = len(args), len(after) + len(near)
    lanes = lambda v: math.prod(v.shape[:-1]) * -(-v.shape[-1] // 128) * 128 * v.dtype.itemsize
    need = sum(map(lanes, [*args, *outs, *free, *scratch]))

    def whole(*refs):
        refs = list(refs)
        take = lambda k: [refs.pop(0) for _ in range(k)]
        ins, _, saved = take(count), take(skip), take(len(spill))
        targets, rest, places = take(len(outs)), take(len(free) + len(kept)), take(len(spill))
        own, landed, made = take(len(scratch)), take(len(far)), take(len(outs))
        in_sems, out_sems = refs
        operands = [In(v) for v in ins]
        for k, i in enumerate(far):
            operands[i] = In(landed[k], pltpu.make_async_copy(ins[i], landed[k], in_sems.at[k]))
        pairs = [*zip(made, targets), *zip(saved, places)]
        copies = [pltpu.make_async_copy(v, t, out_sems.at[k]) for k, (v, t) in enumerate(pairs)]
        gone = [False] * len(made)

        def go(ref):
            k = next(i for i, v in enumerate(made) if v is ref)
            gone[k] = True
            copies[k].start()

        for copy in copies[len(made) :]:
            copy.start()
        kernel(operands, [*made, *rest], go, *own)
        for k, copy in enumerate(copies[: len(made)]):
            if not gone[k]:
                copy.start()
        for v in operands:
            v()
        for copy in copies:
            copy.wait()

    specs = [VMEM] * count
    for i in far:
        specs[i] = HBM
    memory = lambda space, values: [space(v.shape, v.dtype) for v in values]
    return pl.pallas_call(
        whole,
        out_shape=tuple(
            [*memory(pltpu.HBM, outs), *free, *memory(pltpu.VMEM, kept), *memory(pltpu.HBM, spill)]
        ),
        in_specs=specs + [ANY] * len(after) + [VMEM] * (len(near) + len(spill)),
        out_specs=tuple([HBM] * len(outs) + [VMEM] * (len(free) + len(kept)) + [HBM] * len(spill)),
        scratch_shapes=[
            *scratch,
            *memory(pltpu.VMEM, [args[i] for i in far]),
            *memory(pltpu.VMEM, outs),
            pltpu.SemaphoreType.DMA((max(1, len(far)),)),
            pltpu.SemaphoreType.DMA((max(1, len(outs) + len(spill)),)),
        ],
        compiler_params=pltpu.CompilerParams(vmem_limit_bytes=min(56 << 20, need + (SPARE << 20))),
        cost_estimate=pl.CostEstimate(flops=int(flops), bytes_accessed=0, transcendentals=0),
        name=name,
    )(*args, *after, *near, *spill)


def dot(a, b):
    return jnp.dot(a, b, preferred_element_type=F32)


def dot_nt(a, b):
    return lax.dot_general(a, b, (((1,), (1,)), ((), ())), preferred_element_type=F32)


def dot_tn(a, b):
    return lax.dot_general(a, b, (((0,), (0,)), ((), ())), preferred_element_type=F32)


def later(v):
    row = lax.broadcasted_iota(jnp.int32, v.shape, 0)
    return jnp.where(row == 0, 0.0, pltpu.roll(v, 1, 0))


def sooner(v):
    rows = v.shape[0]
    row = lax.broadcasted_iota(jnp.int32, v.shape, 0)
    return jnp.where(row == rows - 1, 0.0, pltpu.roll(v, rows - 1, 0))


def inv_rms(v):
    return lax.rsqrt(jnp.mean(v * v, axis=-1, keepdims=True) + EPS)


def in_two(v):
    high = v.astype(BF16).astype(F32)
    return jnp.concatenate([high, v - high], axis=0).astype(BF16)


def joined(tail):
    rows = tail.shape[0] // 2
    return tail[:rows].astype(F32) + tail[rows:].astype(F32)


def picker(shape, me, c):
    row = lax.broadcasted_iota(jnp.int32, shape, 0)
    col = lax.broadcasted_iota(jnp.int32, shape, 1)
    return jnp.where(row == col + me * c, 1.0, 0.0).astype(BF16)


def mid_kernel(n, c, chans, ins, outs, go):
    me = lax.axis_index("seq")
    cot, w = ins[:2]
    stays = outs[n:]
    g, w = cot()[...], w()
    for k in range(n):
        at = pl.multiple_of(lax.rem(me + k, n) * c, c & -c)
        rows = jnp.concatenate([w[pl.ds(at, c), :], w[pl.ds(chans + at, c), :]], axis=0)
        outs[k][...] = dot_nt(g, rows).astype(BF16)
    for v, stay in zip(ins, stays):
        stay[...] = v()[...]


def conv_kernel_fwd(n, c, chans, ins, outs, go, xs):
    me = lax.axis_index("seq")
    blocks, (taps, gain) = ins[:n], ins[n:]
    pooled_msg, pooled, conv_out, nin, rone = outs
    rows = blocks[0].ref.shape[0]
    gains = gain()[...]
    for k in range(n):
        at = pl.multiple_of(lax.rem(me - k + n, n) * rows, rows)
        v = blocks[k]()[...]
        xs[pl.ds(at, rows), :] = v
        for h in range(2):
            f = v[:, h * chans : (h + 1) * chans].astype(F32)
            r = inv_rms(f)
            rone[pl.ds(at, rows), h : h + 1] = r
            nin[pl.ds(at, rows), h * chans : (h + 1) * chans] = (f * r * gains).astype(BF16)
    nin = nin
    xe, xo = nin[:, :chans], nin[:, chans:]
    taps = taps()
    k0, k1, k2, k3, k4 = (taps[k * c : (k + 1) * c, :] for k in range(5))
    even = dot_nt(xe, k2) + dot_nt(xo, k3) + later(dot_nt(xe, k0) + dot_nt(xo, k1)) + sooner(dot_nt(xe, k4))
    odd = dot_nt(xe, k1) + dot_nt(xo, k2) + later(dot_nt(xo, k0)) + sooner(dot_nt(xe, k3) + dot_nt(xo, k4))
    conv = jnp.concatenate([even, odd], axis=1)
    pick = picker((chans, c), me, c)
    own = jnp.concatenate([dot(xs[:, :chans], pick), dot(xs[:, chans:], pick)], axis=1)
    total = own + conv * jax.nn.sigmoid(conv)
    pooled_msg[...] = total.astype(BF16)
    conv_out[...] = conv
    pooled[...] = total


def qkv_kernel(n, c, chans, ins, outs, go):
    me = lax.axis_index("seq")
    blocks, mids = ins[:n], ins[n : 2 * n]
    gains, cot, w = ins[2 * n :]
    nmt, rtwo, *msgs, qkv, part = outs
    squares = 0.0
    for v in blocks:
        v = v()[...].astype(F32)
        squares = squares + jnp.sum(v * v, axis=1, keepdims=True)
    r = lax.rsqrt(squares * (1.0 / (2 * chans)) + EPS)
    rtwo[...] = r
    gains = gains()
    for k in range(n):
        b = lax.rem(me - k + n, n)
        v = blocks[k]()[...].astype(F32) * r * gains[pl.ds(b, 1), :]
        t = v.T.astype(BF16)
        for h in range(2):
            at = pl.multiple_of(h * chans + b * c, c & -c)
            nmt[pl.ds(at, c), :] = t[h * c : (h + 1) * c, :]
    go(nmt)
    half, wide = mids[0].ref.shape
    q = dot_tn(nmt[...], w()[...])
    row = jnp.sum(q * cot()[...].astype(F32), axis=1, keepdims=True)
    row = jnp.broadcast_to(row, (row.shape[0], 128)).T[:8, :]
    part[...] = row
    if msgs:
        if half < wide:
            row = jnp.concatenate([row, jnp.zeros((8, wide - half), F32)], axis=1)
        for k in range(n):
            msgs[k][:half, :] = mids[k]()[...]
            msgs[k][half:, :] = in_two(row)
            go(msgs[k])
    qkv[...] = q.astype(BF16)


def back_kernel(n, c, chans, m, ins, outs, go, evens, odds, whole):
    seq_at = lax.axis_index("seq")
    core = lax.rem(lax.axis_index("dp"), 2)
    mids, parts = ins[:n], ins[n:-8]
    pooled, rtwo, conv_out, gmid, nin, gin, rone, taps = ins[-8:]
    send, keep, *msgs = outs
    half = rtwo().shape[0]
    r = rtwo()[...]
    atwo = pooled()[...] * r
    conv = conv_out()[...]
    sig = jax.nn.sigmoid(conv)
    slope = sig * (1.0 + conv * (1.0 - sig))
    gains = gmid()[pl.ds(seq_at, 1), :]
    mid, rowsum = 0.0, 0.0
    for v in mids:
        mid = mid + v()[:half, :].astype(F32)
    if parts:
        for v in parts:
            rowsum = rowsum + v()[...]
    else:
        for v in mids:
            rowsum = rowsum + joined(v()[half:, :])[:, :half]
    mean = jnp.concatenate([rowsum] * 16, axis=0).T[:, :1] * (1.0 / (2 * chans))
    section = r * (gains * mid - atwo * mean)
    cg = section * slope
    cg = cg.astype(BF16).astype(F32)
    ge, gd = cg[:, :c], cg[:, c:]
    bf = lambda v: v.astype(BF16)
    g0, gp, gm = bf(ge), bf(sooner(ge)), bf(later(ge))
    o0, op, om = bf(gd), bf(sooner(gd)), bf(later(gd))
    evens[...] = jnp.concatenate((gp, o0, g0, om, gm), axis=1)
    odds[...] = jnp.concatenate((op, gp, o0, g0, om), axis=1)
    wide, rows = chans // 2, 5 * c // (m // 2)
    nin = nin()
    for out, which in ((send, 1 - core), (keep, core)):
        at = pl.multiple_of(which * wide, wide & -wide)
        kg = dot_tn(evens[...], nin[:, pl.ds(at, wide)]) + dot_tn(odds[...], nin[:, pl.ds(chans + at, wide)])
        for q in range(m // 2):
            out[q] = kg[q * rows : (q + 1) * rows, :].astype(out.dtype)
        go(out)
    width = 2 * chans
    block = half // n
    gin, rone, taps = gin()[...], rone()[...], taps()[...]
    pick = picker((chans, c), seq_at, c)
    grad = section.astype(BF16)
    acc = 0.0
    lane = lax.broadcasted_iota(jnp.int32, (half, 128), 1)
    means = jnp.zeros((half, 128), F32)
    for h, g in ((0, evens), (1, odds)):
        ng = dot(g[...], taps)
        aone = nin[:, h * chans : (h + 1) * chans].astype(F32) / gin
        acc = acc + jnp.sum(ng * aone, axis=0, keepdims=True)
        placed = dot_nt(grad[:, h * c : (h + 1) * c], pick)
        means = jnp.where(lane == h, jnp.mean(placed * aone, axis=1, keepdims=True), means)
        total = (placed + rone[:, h : h + 1] * gin * ng).astype(BF16)
        whole[:, h * chans : (h + 1) * chans] = total
    whole[:, width : width + 128] = means.astype(BF16)
    mid = jnp.sum(mid * atwo, axis=0, keepdims=True)
    short = -2 * c % 128
    if short:
        mid = jnp.concatenate([mid, jnp.zeros((1, short), F32)], axis=1)
    line = lax.broadcasted_iota(jnp.int32, (16, 128), 0)
    gains = jnp.zeros((16, 128), F32)
    vector = jnp.concatenate([acc, mid], axis=1)
    for i in range(vector.shape[1] // 128):
        gains = jnp.where(line == i, vector[:, i * 128 : (i + 1) * 128], gains)
    gains = in_two(gains)
    for k in range(n):
        at = pl.multiple_of(lax.rem(seq_at + k, n) * block, block)
        msgs[k][:, : width + 128] = whole[pl.ds(at, block), :]
        msgs[k][:, width + 128 :] = jnp.zeros((block, 128), BF16)
        msgs[k][:32, width + 128 :] = gains
        go(msgs[k])


def weight_kernel(m, scale, ins, outs, go):
    nms, cots = ins
    nms, cots = nms(), cots()
    half = nms.shape[2]
    total = dot(nms[0], cots[:half, :])
    for b in range(1, m):
        total = total + dot(nms[b], cots[b * half : (b + 1) * half, :])
    total = (total * scale).astype(BF16)
    for q in range(m // 2):
        outs[0][q] = total


def split_kernel(q, ins, outs, go):
    keep, recv = ins
    me = lax.axis_index("dp") // 2
    keep, recv = keep(), recv()
    for k in [*range(1, q), 0]:
        out = outs[k - 1]
        out[...] = (keep[me ^ k] + recv[me ^ k].astype(F32)).astype(out.dtype)


def finish_kernel(n, chans, scale, ins, outs, go):
    total = ins[0]()[...]
    for r in ins[1:-1]:
        total = total + r()[...].astype(F32)
    rows, wide = total.shape
    outs[0][:rows, :] = (total * scale).astype(BF16)
    gains = ins[-1]()
    pieces, count = wide // 128, chans // 128
    both = gains[0]
    for b in range(1, n):
        both = both + gains[b]
    line = lax.broadcasted_iota(jnp.int32, (8, wide), 0)
    tail = jnp.zeros((8, wide), F32)
    wanted = [(i, both, i * pieces) for i in range(2)] + [(2 + b, gains[b], count) for b in range(n)]
    for i, source, first in wanted:
        row = jnp.concatenate([source[first + j : first + j + 1, :] for j in range(pieces)], axis=1)
        tail = jnp.where(line == i, row, tail)
    outs[0][rows:, :] = in_two(tail * scale)


def half_kernel(q, ins, outs, go):
    me = lax.axis_index("dp") // 2
    out = outs[0]
    rows = ins[0].ref.shape[0] - 16
    tail = 0.0
    for k in range(q):
        at = pl.multiple_of((me ^ k) * rows, rows & -rows)
        out[pl.ds(at, rows), :] = ins[k]()[:rows, :]
        tail = tail + joined(ins[k]()[rows:, :])
    out[q * rows :, :] = in_two(tail)


def place_kernel(n, c, ins, outs, go):
    core = lax.rem(lax.axis_index("dp"), 2)
    mine, other = ins
    taps, gain_in, gain_mid = outs
    rows, wide = taps.shape[0], mine.ref.shape[1]
    total = 0.0
    for v, which in ((mine, core), (other, 1 - core)):
        side = pl.multiple_of(which * wide, wide & -wide)
        taps[:, pl.ds(side, wide)] = v()[:rows, :]
        total = total + joined(v()[rows:, :])
    gain_in[...] = total[:2, :]
    gain_mid[...] = total[2 : 2 + n, : 2 * c]


def hand_kernel(ins, outs, go):
    outs[0][...] = ins[0]()[...]


def weave_kernel(ins, outs, go):
    core = lax.rem(lax.axis_index("dp"), 2)
    mine, other = ins
    for v, which in ((mine, core), (other, 1 - core)):
        for q in range(v.ref.shape[0]):
            outs[0][q, which] = v()[q]


def input_kernel(n, chans, ins, outs, go):
    me = lax.axis_index("seq")
    got, own = ins[:n], ins[n]
    out, gains = outs
    total = got[0]()[:, : 2 * chans + 128].astype(F32)
    for v in got[1:]:
        total = total + v()[:, : 2 * chans + 128].astype(F32)
    for k in range(n):
        gains[lax.rem(me - k + n, n)] = joined(got[k]()[:32, 2 * chans + 128 :])
    for h in range(2):
        x = own()[:, h * chans : (h + 1) * chans].astype(F32)
        a = x * inv_rms(x)
        t = total[:, h * chans : (h + 1) * chans]
        mean = total[:, 2 * chans + h : 2 * chans + h + 1]
        v = t - a * (jnp.mean(t * a, axis=-1, keepdims=True) - mean)
        out[:, h * chans : (h + 1) * chans] = v.astype(BF16)


def body(section_input, conv_kernel, qkv_weight, gain_in, gain_mid, qkv_cotangent):
    x = section_input[0]
    cot = qkv_cotangent[0]
    length, chans = x.shape
    c = conv_kernel.shape[2]
    width, cols = qkv_weight.shape
    n, m = lax.axis_size("seq"), lax.axis_size("dp")
    half = length // 2 * n
    scale = 1.0 / math.sqrt(m * half)
    shift = lambda v, k: lax.ppermute(v, "seq", [(i, (i + k) % n) for i in range(n)])
    from_ring = lambda v: [v] + [shift(v, k) for k in range(1, n)]
    across = lambda v, k: lax.ppermute(v, "dp", [(i, i ^ k) for i in range(m)])
    same_core = [[i for i in range(m) if i % 2 == core] for core in range(2)]
    chips = m // 2
    rows, wide = 5 * c // chips, chans // 2

    taps = conv_kernel.transpose(0, 2, 1)
    own = x.reshape(length // 2, width)
    xs = from_ring(own)
    gin = gain_in.reshape(1, chans)
    gmid = gain_mid.reshape(2, n, c).transpose(1, 0, 2).reshape(n, 2 * c)
    cots = lax.all_gather(cot, "dp", axis=0, tiled=True)
    used = [cot, qkv_weight, taps.reshape(5 * c, chans), gin, gmid]
    held = call(
        functools.partial(mid_kernel, n, c, chans),
        [*map(Far, used)],
        kept=[shaped((half, 2 * c), BF16)] * n + [shaped(v.shape, v.dtype) for v in used],
        name="mid_parts",
    )
    mid_msgs = held[:n]
    cot, weight, taps, gin, gmid = held[n:]
    pooled_msg, *states = call(
        functools.partial(conv_kernel_fwd, n, c, chans),
        [*xs, taps, gin],
        free=[shaped((half, 2 * c), BF16)],
        kept=[
            shaped((half, 2 * c), F32),
            shaped((half, 2 * c), F32),
            shaped((half, width), BF16),
            shaped((half, 2), F32),
        ],
        scratch=[pltpu.VMEM((half, width), BF16)],
        name="conv_forward",
    )
    blocks = from_ring(pooled_msg)
    rides = half <= 2 * c
    nmt, rtwo, *tailed, qkv, part, pooled, conv_out, nin, rone = call(
        functools.partial(qkv_kernel, n, c, chans),
        [*blocks, *mid_msgs, gmid, cot, weight],
        outs=[shaped((width, half), BF16), shaped((half, 1), F32)] + [shaped((half + 16, 2 * c), BF16)] * (n * rides),
        free=[shaped((half, cols), BF16), shaped((8, half), F32)],
        spill=states,
        name="qkv",
    )
    mid_msgs = tailed if rides else mid_msgs
    mids = [Far(mid_msgs[0])] + [shift(mid_msgs[k], k) for k in range(1, n)]
    parts = [] if rides else from_ring(part)
    nms = lax.all_to_all(nmt.reshape(m, width // m, half), "dp", 0, 0, tiled=True)
    (wshare,) = call(
        functools.partial(weight_kernel, m, scale),
        [nms, Far(cots)],
        outs=[shaped((chips, width // m, cols), BF16)],
        name="weight_share",
    )
    whalf = lax.all_to_all(wshare, "dp", 0, 0, axis_index_groups=same_core, tiled=True)
    send, keep, *msgs = call(
        functools.partial(back_kernel, n, c, chans, m),
        [
            *mids,
            *parts,
            *map(Far, [pooled, rtwo, conv_out]),
            gmid,
            Far(nin),
            gin,
            Far(rone),
            taps,
        ],
        outs=[
            shaped((chips, rows, wide), BF16),
            shaped((chips, rows, wide), F32),
        ]
        + [shaped((half // n, width + 256), BF16)] * n,
        after=[wshare],
        scratch=[
            pltpu.VMEM((half, 5 * c), BF16),
            pltpu.VMEM((half, 5 * c), BF16),
            pltpu.VMEM((half, width + 128), BF16),
        ],
        flops=WAIT,
        name="conv_backward",
    )
    got = [msgs[0]] + [shift(msgs[k], k) for k in range(1, n)]
    input_grad, gains = call(
        functools.partial(input_kernel, n, chans),
        [*got, own],
        free=[shaped((length // 2, width), BF16), shaped((n, 16, 128), F32)],
        name="input_grad",
    )
    *split, keep_sum = call(
        functools.partial(split_kernel, chips),
        [Far(keep), across(send, 1)],
        free=[shaped((rows, wide), BF16)] * (chips - 1),
        kept=[shaped((rows, wide), F32)],
        name="core_sum",
    )
    if rows % 16 == 0 and n <= 6:
        (kshare,) = call(
            functools.partial(finish_kernel, n, chans, scale),
            [keep_sum] + [across(split[k - 1], 2 * k) for k in range(1, chips)] + [gains],
            free=[shaped((rows + 16, wide), BF16)],
            name="chip_sum",
        )
        kshares = [kshare] + [across(kshare, k) for k in range(2, m, 2)]
        last = kshares[1]
        (mine,) = call(
            functools.partial(half_kernel, chips),
            kshares,
            free=[shaped((5 * c + 16, wide), BF16)],
            name="kernel_grad_half",
        )
        taps_grad, gain_in_grad, gain_mid_grad = call(
            functools.partial(place_kernel, n, c),
            [mine, across(mine, 1)],
            free=[shaped((5 * c, chans), BF16), shaped((2, wide), F32), shaped((n, 2 * c), F32)],
            name="kernel_grad",
        )
    else:
        core = lax.axis_index("dp") % 2
        both = jnp.stack([keep, send.astype(F32)])
        both = jnp.where(core == 0, both, both[::-1]).transpose(1, 2, 0, 3).reshape(5 * c, chans)
        both, gains = lax.psum((both, gains), "dp")
        taps_grad, gains = (both * scale).astype(BF16), gains * scale
        gain_in_grad = jnp.sum(gains[:, : chans // 128], axis=0)
        gain_mid_grad = gains[:, chans // 128 :].reshape(n, -1)[:, : 2 * c]
        last = gains
    (whalf,) = call(hand_kernel, [whalf], free=[shaped(whalf.shape, BF16)], after=[last], name="weight_grad_half")
    (weight_grad,) = call(
        weave_kernel,
        [whalf, across(whalf, 1)],
        free=[shaped((chips, 2, width // m, cols), BF16)],
        name="weight_grad",
    )
    return (
        qkv[None],
        input_grad.reshape(1, length, chans),
        taps_grad.reshape(5, c, chans).transpose(0, 2, 1),
        gain_in_grad.reshape(chans),
        gain_mid_grad.reshape(n, 2, c).transpose(1, 0, 2).reshape(width),
        weight_grad.reshape(width, cols),
    )


def solution(mesh):
    placed = (
        P("dp", "seq", None),
        P(None, None, "seq"),
        P(None, "seq"),
        P(),
        P(),
        P("dp", None, "seq"),
    )
    return jax.shard_map(
        body,
        mesh=mesh,
        in_specs=placed,
        out_specs=(
            P("dp", None, "seq"),
            P("dp", "seq", None),
            P(None, None, "seq"),
            P(),
            P(),
            P(None, "seq"),
        ),
        check_vma=False,
    )
```

```python
import functools
import math

import jax
import jax.numpy as jnp
from jax import lax
from jax.experimental import pallas as pl
from jax.experimental.pallas import tpu as pltpu
from jax.sharding import PartitionSpec as P

EPS = 1e-06
WAIT = 4e10
SPARE = 12
F32 = jnp.float32
BF16 = jnp.bfloat16
ANY = pl.BlockSpec(memory_space=pl.ANY)
HBM = pl.BlockSpec(memory_space=pltpu.HBM)
VMEM = pl.BlockSpec(memory_space=pltpu.VMEM)


class In:
    def __init__(self, ref, copy=None):
        self.ref, self.copy = ref, copy
        if copy is not None:
            copy.start()

    def __call__(self):
        if self.copy is not None:
            self.copy.wait()
            self.copy = None
        return self.ref


def shaped(shape, dtype):
    return jax.ShapeDtypeStruct(shape, dtype)


class Far:
    def __init__(self, value):
        self.value = value


def call(kernel, args, outs=(), free=(), kept=(), after=(), near=(), spill=(), fetch=(), scratch=(), flops=0, name=None):
    within = lambda v: pltpu.with_memory_space_constraint(v, pltpu.VMEM)
    near, spill = [within(v) for v in near], [within(v) for v in spill]
    fetch = [pltpu.with_memory_space_constraint(v, pltpu.HBM) for v in fetch]
    after = [pltpu.with_memory_space_constraint(v, pltpu.HBM) for v in after]
    far = [i for i, v in enumerate(args) if isinstance(v, Far)]
    args = [pltpu.with_memory_space_constraint(v.value, pltpu.HBM) if isinstance(v, Far) else v for v in args]
    count, skip = len(args), len(after) + len(near)
    lanes = lambda v: math.prod(v.shape[:-1]) * -(-v.shape[-1] // 128) * 128 * v.dtype.itemsize
    need = sum(map(lanes, [*args, *outs, *free, *scratch]))

    def whole(*refs):
        refs = list(refs)
        take = lambda k: [refs.pop(0) for _ in range(k)]
        ins, _, saved, fetched = take(count), take(skip), take(len(spill)), take(len(fetch))
        targets, rest, places, nears = take(len(outs)), take(len(free) + len(kept)), take(len(spill)), take(len(fetch))
        own, landed, made = take(len(scratch)), take(len(far)), take(len(outs))
        in_sems, out_sems = refs
        operands = [In(v) for v in ins]
        for k, i in enumerate(far):
            operands[i] = In(landed[k], pltpu.make_async_copy(ins[i], landed[k], in_sems.at[k]))
        pairs = [*zip(made, targets), *zip(saved, places), *zip(fetched, nears)]
        copies = [pltpu.make_async_copy(v, t, out_sems.at[k]) for k, (v, t) in enumerate(pairs)]
        gone = [False] * len(made)

        def go(ref):
            k = next(i for i, v in enumerate(made) if v is ref)
            gone[k] = True
            copies[k].start()

        for copy in copies[len(made) :]:
            copy.start()
        kernel(operands, [*made, *rest], go, *own)
        for k, copy in enumerate(copies[: len(made)]):
            if not gone[k]:
                copy.start()
        for v in operands:
            v()
        for copy in copies:
            copy.wait()

    specs = [VMEM] * count
    for i in far:
        specs[i] = HBM
    memory = lambda space, values: [space(v.shape, v.dtype) for v in values]
    return pl.pallas_call(
        whole,
        out_shape=tuple(
            [*memory(pltpu.HBM, outs), *free, *memory(pltpu.VMEM, kept), *memory(pltpu.HBM, spill)]
            + memory(pltpu.VMEM, fetch)
        ),
        in_specs=specs + [HBM] * len(after) + [VMEM] * (len(near) + len(spill)) + [HBM] * len(fetch),
        out_specs=tuple([HBM] * len(outs) + [VMEM] * (len(free) + len(kept)) + [HBM] * len(spill) + [VMEM] * len(fetch)),
        scratch_shapes=[
            *scratch,
            *memory(pltpu.VMEM, [args[i] for i in far]),
            *memory(pltpu.VMEM, outs),
            pltpu.SemaphoreType.DMA((max(1, len(far)),)),
            pltpu.SemaphoreType.DMA((max(1, len(outs) + len(spill) + len(fetch)),)),
        ],
        compiler_params=pltpu.CompilerParams(vmem_limit_bytes=min(56 << 20, need + (SPARE << 20))),
        cost_estimate=pl.CostEstimate(flops=int(flops), bytes_accessed=0, transcendentals=0),
        name=name,
    )(*args, *after, *near, *spill, *fetch)


def gate(value, after, space=pltpu.VMEM):
    spec = pl.BlockSpec(memory_space=space)
    return pl.pallas_call(
        lambda *_: None,
        out_shape=space(value.shape, value.dtype),
        in_specs=[spec, ANY],
        out_specs=spec,
        input_output_aliases={0: 0},
        compiler_params=pltpu.CompilerParams(vmem_limit_bytes=SPARE << 20),
        cost_estimate=pl.CostEstimate(flops=0, bytes_accessed=0, transcendentals=0),
        name="gate",
    )(pltpu.with_memory_space_constraint(value, space), after)


def dot(a, b):
    return jnp.dot(a, b, preferred_element_type=F32)


def dot_nt(a, b):
    return lax.dot_general(a, b, (((1,), (1,)), ((), ())), preferred_element_type=F32)


def dot_tn(a, b):
    return lax.dot_general(a, b, (((0,), (0,)), ((), ())), preferred_element_type=F32)


def later(v):
    row = lax.broadcasted_iota(jnp.int32, v.shape, 0)
    return jnp.where(row == 0, 0.0, pltpu.roll(v, 1, 0))


def sooner(v):
    rows = v.shape[0]
    row = lax.broadcasted_iota(jnp.int32, v.shape, 0)
    return jnp.where(row == rows - 1, 0.0, pltpu.roll(v, rows - 1, 0))


def inv_rms(v):
    return lax.rsqrt(jnp.mean(v * v, axis=-1, keepdims=True) + EPS)


def in_two(v):
    high = v.astype(BF16).astype(F32)
    return jnp.concatenate([high, v - high], axis=0).astype(BF16)


def joined(tail):
    rows = tail.shape[0] // 2
    return tail[:rows].astype(F32) + tail[rows:].astype(F32)


def picker(shape, me, c):
    row = lax.broadcasted_iota(jnp.int32, shape, 0)
    col = lax.broadcasted_iota(jnp.int32, shape, 1)
    return jnp.where(row == col + me * c, 1.0, 0.0).astype(BF16)


def mid_kernel(n, c, chans, ins, outs, go):
    me = lax.axis_index("seq")
    cot, w = ins[:2]
    stays = outs[n:]
    g, w = cot()[...], w()
    for k in range(n):
        at = pl.multiple_of(lax.rem(me + k, n) * c, c & -c)
        rows = jnp.concatenate([w[pl.ds(at, c), :], w[pl.ds(chans + at, c), :]], axis=0)
        outs[k][...] = dot_nt(g, rows).astype(BF16)
    for v, stay in zip(ins, stays):
        stay[...] = v()[...]


def conv_kernel_fwd(n, c, chans, ins, outs, go, xs):
    me = lax.axis_index("seq")
    blocks, (taps, gain) = ins[:n], ins[n:]
    pooled_msg, pooled, conv_out, nin, rone = outs
    rows = blocks[0].ref.shape[0]
    gains = gain()[...]
    for k in range(n):
        at = pl.multiple_of(lax.rem(me - k + n, n) * rows, rows)
        v = blocks[k]()[...]
        xs[pl.ds(at, rows), :] = v
        for h in range(2):
            f = v[:, h * chans : (h + 1) * chans].astype(F32)
            r = inv_rms(f)
            rone[pl.ds(at, rows), h : h + 1] = r
            nin[pl.ds(at, rows), h * chans : (h + 1) * chans] = (f * r * gains).astype(BF16)
    nin = nin
    xe, xo = nin[:, :chans], nin[:, chans:]
    taps = taps()
    k0, k1, k2, k3, k4 = (taps[k * c : (k + 1) * c, :] for k in range(5))
    even = dot_nt(xe, k2) + dot_nt(xo, k3) + later(dot_nt(xe, k0) + dot_nt(xo, k1)) + sooner(dot_nt(xe, k4))
    odd = dot_nt(xe, k1) + dot_nt(xo, k2) + later(dot_nt(xo, k0)) + sooner(dot_nt(xe, k3) + dot_nt(xo, k4))
    conv = jnp.concatenate([even, odd], axis=1)
    pick = picker((chans, c), me, c)
    own = jnp.concatenate([dot(xs[:, :chans], pick), dot(xs[:, chans:], pick)], axis=1)
    total = own + conv * jax.nn.sigmoid(conv)
    pooled_msg[...] = total.astype(BF16)
    conv_out[...] = conv
    pooled[...] = total


def qkv_kernel(n, c, chans, ins, outs, go):
    me = lax.axis_index("seq")
    blocks, mids = ins[:n], ins[n : 2 * n]
    gains, cot, w = ins[2 * n :]
    nmt, rtwo, *msgs, qkv, part = outs
    squares = 0.0
    for v in blocks:
        v = v()[...].astype(F32)
        squares = squares + jnp.sum(v * v, axis=1, keepdims=True)
    r = lax.rsqrt(squares * (1.0 / (2 * chans)) + EPS)
    rtwo[...] = r
    gains = gains()
    for k in range(n):
        b = lax.rem(me - k + n, n)
        v = blocks[k]()[...].astype(F32) * r * gains[pl.ds(b, 1), :]
        t = v.T.astype(BF16)
        for h in range(2):
            at = pl.multiple_of(h * chans + b * c, c & -c)
            nmt[pl.ds(at, c), :] = t[h * c : (h + 1) * c, :]
    go(nmt)
    half, wide = mids[0].ref.shape
    q = dot_tn(nmt[...], w()[...])
    row = jnp.sum(q * cot()[...].astype(F32), axis=1, keepdims=True)
    row = jnp.broadcast_to(row, (row.shape[0], 128)).T[:8, :]
    part[...] = row
    if msgs:
        if half < wide:
            row = jnp.concatenate([row, jnp.zeros((8, wide - half), F32)], axis=1)
        for k in range(n):
            msgs[k][:half, :] = mids[k]()[...]
            msgs[k][half:, :] = in_two(row)
            go(msgs[k])
    qkv[...] = q.astype(BF16)


def back_kernel(n, c, chans, m, ins, outs, go, evens, odds, whole):
    seq_at = lax.axis_index("seq")
    core = lax.rem(lax.axis_index("dp"), 2)
    mids, parts = ins[:n], ins[n:-8]
    pooled, rtwo, conv_out, gmid, nin, gin, rone, taps = ins[-8:]
    send, keep, *msgs = outs
    half = rtwo().shape[0]
    r = rtwo()[...]
    atwo = pooled()[...] * r
    conv = conv_out()[...]
    sig = jax.nn.sigmoid(conv)
    slope = sig * (1.0 + conv * (1.0 - sig))
    gains = gmid()[pl.ds(seq_at, 1), :]
    mid, rowsum = 0.0, 0.0
    for v in mids:
        mid = mid + v()[:half, :].astype(F32)
    if parts:
        for v in parts:
            rowsum = rowsum + v()[...]
    else:
        for v in mids:
            rowsum = rowsum + joined(v()[half:, :])[:, :half]
    mean = jnp.concatenate([rowsum] * 16, axis=0).T[:, :1] * (1.0 / (2 * chans))
    section = r * (gains * mid - atwo * mean)
    cg = section * slope
    cg = cg.astype(BF16).astype(F32)
    ge, gd = cg[:, :c], cg[:, c:]
    bf = lambda v: v.astype(BF16)
    g0, gp, gm = bf(ge), bf(sooner(ge)), bf(later(ge))
    o0, op, om = bf(gd), bf(sooner(gd)), bf(later(gd))
    evens[...] = jnp.concatenate((gp, o0, g0, om, gm), axis=1)
    odds[...] = jnp.concatenate((op, gp, o0, g0, om), axis=1)
    wide, rows = chans // 2, 5 * c // (m // 2)
    nin = nin()
    for out, which in ((send, 1 - core), (keep, core)):
        at = pl.multiple_of(which * wide, wide & -wide)
        kg = dot_tn(evens[...], nin[:, pl.ds(at, wide)]) + dot_tn(odds[...], nin[:, pl.ds(chans + at, wide)])
        for q in range(m // 2):
            out[q] = kg[q * rows : (q + 1) * rows, :].astype(out.dtype)
        go(out)
    width = 2 * chans
    block = half // n
    gin, rone, taps = gin()[...], rone()[...], taps()[...]
    pick = picker((chans, c), seq_at, c)
    grad = section.astype(BF16)
    acc = 0.0
    lane = lax.broadcasted_iota(jnp.int32, (half, 128), 1)
    means = jnp.zeros((half, 128), F32)
    for h, g in ((0, evens), (1, odds)):
        ng = dot(g[...], taps)
        aone = nin[:, h * chans : (h + 1) * chans].astype(F32) / gin
        acc = acc + jnp.sum(ng * aone, axis=0, keepdims=True)
        placed = dot_nt(grad[:, h * c : (h + 1) * c], pick)
        means = jnp.where(lane == h, jnp.mean(placed * aone, axis=1, keepdims=True), means)
        total = (placed + rone[:, h : h + 1] * gin * ng).astype(BF16)
        whole[:, h * chans : (h + 1) * chans] = total
    whole[:, width : width + 128] = means.astype(BF16)
    mid = jnp.sum(mid * atwo, axis=0, keepdims=True)
    short = -2 * c % 128
    if short:
        mid = jnp.concatenate([mid, jnp.zeros((1, short), F32)], axis=1)
    line = lax.broadcasted_iota(jnp.int32, (16, 128), 0)
    gains = jnp.zeros((16, 128), F32)
    vector = jnp.concatenate([acc, mid], axis=1)
    for i in range(vector.shape[1] // 128):
        gains = jnp.where(line == i, vector[:, i * 128 : (i + 1) * 128], gains)
    gains = in_two(gains)
    for k in range(n):
        at = pl.multiple_of(lax.rem(seq_at + k, n) * block, block)
        msgs[k][:, : width + 128] = whole[pl.ds(at, block), :]
        msgs[k][:, width + 128 :] = jnp.zeros((block, 128), BF16)
        msgs[k][:32, width + 128 :] = gains
        go(msgs[k])


def weight_kernel(m, scale, ins, outs, go):
    core = lax.rem(lax.axis_index("dp"), 2)
    nms, total = ins[0](), 0.0
    for v, which in zip(ins[1:], (core, 1 - core)):
        v = v()
        for q in range(m // 2):
            total = total + dot(nms[2 * q + which], v[q])
    total = (total * scale).astype(BF16)
    for q in range(m // 2):
        outs[0][q] = total


def split_kernel(q, ins, outs, go):
    keep, recv = ins
    me = lax.axis_index("dp") // 2
    keep, recv = keep(), recv()
    for k in [*range(1, q), 0]:
        out = outs[k - 1]
        out[...] = (keep[me ^ k] + recv[me ^ k].astype(F32)).astype(out.dtype)


def finish_kernel(n, chans, scale, ins, outs, go):
    total = ins[0]()[...]
    for r in ins[1:-1]:
        total = total + r()[...].astype(F32)
    rows, wide = total.shape
    outs[0][:rows, :] = (total * scale).astype(BF16)
    gains = ins[-1]()
    pieces, count = wide // 128, chans // 128
    both = gains[0]
    for b in range(1, n):
        both = both + gains[b]
    line = lax.broadcasted_iota(jnp.int32, (8, wide), 0)
    tail = jnp.zeros((8, wide), F32)
    wanted = [(i, both, i * pieces) for i in range(2)] + [(2 + b, gains[b], count) for b in range(n)]
    for i, source, first in wanted:
        row = jnp.concatenate([source[first + j : first + j + 1, :] for j in range(pieces)], axis=1)
        tail = jnp.where(line == i, row, tail)
    outs[0][rows:, :] = in_two(tail * scale)


def half_kernel(q, ins, outs, go):
    me = lax.axis_index("dp") // 2
    out = outs[0]
    rows = ins[0].ref.shape[0] - 16
    tail = 0.0
    for k in range(q):
        at = pl.multiple_of((me ^ k) * rows, rows & -rows)
        out[pl.ds(at, rows), :] = ins[k]()[:rows, :]
        tail = tail + joined(ins[k]()[rows:, :])
    out[q * rows :, :] = in_two(tail)


def place_kernel(n, c, ins, outs, go):
    core = lax.rem(lax.axis_index("dp"), 2)
    mine, other = ins
    taps, gain_in, gain_mid = outs
    rows, wide = taps.shape[0], mine.ref.shape[1]
    total = 0.0
    for v, which in ((mine, core), (other, 1 - core)):
        side = pl.multiple_of(which * wide, wide & -wide)
        taps[:, pl.ds(side, wide)] = v()[:rows, :]
        total = total + joined(v()[rows:, :])
    gain_in[...] = total[:2, :]
    gain_mid[...] = total[2 : 2 + n, : 2 * c]


def weave_kernel(mine, other, *refs):
    core = lax.rem(lax.axis_index("dp"), 2)
    out, sems = refs[-2:]
    copies = []
    for v, which in ((mine, core), (other, 1 - core)):
        for q in range(v.shape[0]):
            copies.append(pltpu.make_async_copy(v.at[q], out.at[q, which], sems.at[len(copies)]))
    for copy in copies:
        copy.start()
    for copy in copies:
        copy.wait()


def input_kernel(n, chans, ins, outs, go):
    me = lax.axis_index("seq")
    got, own = ins[:n], ins[n]
    out, gains = outs
    total = got[0]()[:, : 2 * chans + 128].astype(F32)
    for v in got[1:]:
        total = total + v()[:, : 2 * chans + 128].astype(F32)
    for k in range(n):
        gains[lax.rem(me - k + n, n)] = joined(got[k]()[:32, 2 * chans + 128 :])
    for h in range(2):
        x = own()[:, h * chans : (h + 1) * chans].astype(F32)
        a = x * inv_rms(x)
        t = total[:, h * chans : (h + 1) * chans]
        mean = total[:, 2 * chans + h : 2 * chans + h + 1]
        v = t - a * (jnp.mean(t * a, axis=-1, keepdims=True) - mean)
        out[:, h * chans : (h + 1) * chans] = v.astype(BF16)


def body(section_input, conv_kernel, qkv_weight, gain_in, gain_mid, qkv_cotangent):
    x = section_input[0]
    cot = qkv_cotangent[0]
    length, chans = x.shape
    c = conv_kernel.shape[2]
    width, cols = qkv_weight.shape
    n, m = lax.axis_size("seq"), lax.axis_size("dp")
    half = length // 2 * n
    scale = 1.0 / math.sqrt(m * half)
    shift = lambda v, k: lax.ppermute(v, "seq", [(i, (i + k) % n) for i in range(n)])
    from_ring = lambda v: [v] + [shift(v, k) for k in range(1, n)]
    across = lambda v, k: lax.ppermute(v, "dp", [(i, i ^ k) for i in range(m)])
    same_core = [[i for i in range(m) if i % 2 == core] for core in range(2)]
    chips = m // 2
    rows, wide = 5 * c // chips, chans // 2

    taps_rows = conv_kernel.transpose(0, 2, 1).reshape(5 * c, chans)
    own = x.reshape(length // 2, width)
    xs = from_ring(own)
    gin = gain_in.reshape(1, chans)
    gmid = gain_mid.reshape(2, n, c).transpose(1, 0, 2).reshape(n, 2 * c)
    cots = jnp.broadcast_to(cot[None], (chips, *cot.shape))
    cots = lax.all_to_all(cots, "dp", 0, 0, axis_index_groups=same_core, tiled=True)
    used = [cot, qkv_weight, taps_rows, gin, gmid]
    held = call(
        functools.partial(mid_kernel, n, c, chans),
        [*map(Far, used)],
        kept=[shaped((half, 2 * c), BF16)] * n + [shaped(v.shape, v.dtype) for v in used],
        flops=WAIT,
        name="mid_parts",
    )
    mid_msgs = held[:n]
    cot, weight, taps, gin, gmid = held[n:]
    pooled_msg, *states = call(
        functools.partial(conv_kernel_fwd, n, c, chans),
        [*xs, taps, gin],
        free=[shaped((half, 2 * c), BF16)],
        kept=[
            shaped((half, 2 * c), F32),
            shaped((half, 2 * c), F32),
            shaped((half, width), BF16),
            shaped((half, 2), F32),
        ],
        scratch=[pltpu.VMEM((half, width), BF16)],
        name="conv_forward",
    )
    blocks = from_ring(pooled_msg)
    rides = half <= 2 * c
    nmt, rtwo, *tailed, qkv, part, pooled, conv_out, nin, rone = call(
        functools.partial(qkv_kernel, n, c, chans),
        [*blocks, *mid_msgs, gmid, cot, weight],
        outs=[shaped((width, half), BF16), shaped((half, 1), F32)] + [shaped((half + 16, 2 * c), BF16)] * (n * rides),
        free=[shaped((half, cols), BF16), shaped((8, half), F32)],
        spill=states,
        name="qkv",
    )
    cots = gate(cots, nmt, pltpu.HBM)
    mid_msgs = tailed if rides else mid_msgs
    mids = [mid_msgs[0]] + [shift(mid_msgs[k], k) for k in range(1, n)]
    parts = [] if rides else from_ring(part)
    nms = lax.all_to_all(nmt.reshape(m, width // m, half), "dp", 0, 0, tiled=True)
    (wshare,) = call(
        functools.partial(weight_kernel, m, scale),
        [nms, Far(cots), Far(across(cots, 1))],
        outs=[shaped((chips, width // m, cols), BF16)],
        name="weight_share",
    )
    whalf = lax.all_to_all(wshare, "dp", 0, 0, axis_index_groups=same_core, tiled=True)
    send, keep, *msgs = call(
        functools.partial(back_kernel, n, c, chans, m),
        [
            Far(mids[0]),
            *mids[1:],
            *parts,
            *map(Far, [pooled, rtwo, conv_out]),
            gmid,
            Far(nin),
            gin,
            Far(rone),
            Far(taps_rows),
        ],
        outs=[
            shaped((chips, rows, wide), BF16),
            shaped((chips, rows, wide), F32),
        ]
        + [shaped((half // n, width + 256), BF16)] * n,
        scratch=[
            pltpu.VMEM((half, 5 * c), BF16),
            pltpu.VMEM((half, 5 * c), BF16),
            pltpu.VMEM((half, width + 128), BF16),
        ],
        after=[wshare],
        flops=WAIT,
        name="conv_backward",
    )
    got = [msgs[0]] + [shift(msgs[k], k) for k in range(1, n)]
    input_grad, gains = call(
        functools.partial(input_kernel, n, chans),
        [*got, own],
        free=[shaped((length // 2, width), BF16), shaped((n, 16, 128), F32)],
        name="input_grad",
    )
    *split, keep_sum = call(
        functools.partial(split_kernel, chips),
        [Far(keep), across(send, 1)],
        free=[shaped((rows, wide), BF16)] * (chips - 1),
        kept=[shaped((rows, wide), F32)],
        name="core_sum",
    )
    if rows % 16 == 0 and n <= 6:
        (kshare,) = call(
            functools.partial(finish_kernel, n, chans, scale),
            [keep_sum] + [across(split[k - 1], 2 * k) for k in range(1, chips)] + [gains],
            free=[shaped((rows + 16, wide), BF16)],
            name="chip_sum",
        )
        whalf = gate(whalf, kshare)
        within = lambda v: pltpu.with_memory_space_constraint(v, pltpu.VMEM)
        weight_grad = pl.pallas_call(
            weave_kernel,
            out_shape=pltpu.HBM((chips, 2, width // m, cols), BF16),
            in_specs=[VMEM, VMEM],
            out_specs=HBM,
            scratch_shapes=[pltpu.SemaphoreType.DMA((m,))],
            compiler_params=pltpu.CompilerParams(vmem_limit_bytes=SPARE << 20),
            cost_estimate=pl.CostEstimate(flops=0, bytes_accessed=0, transcendentals=0),
            name="weight_grad",
        )(within(whalf), within(across(whalf, 1)))
        kshares = [kshare] + [across(kshare, k) for k in range(2, m, 2)]
        (mine,) = call(
            functools.partial(half_kernel, chips),
            kshares,
            free=[shaped((5 * c + 16, wide), BF16)],
            after=[weight_grad],
            name="kernel_grad_half",
        )
        taps_grad, gain_in_grad, gain_mid_grad = call(
            functools.partial(place_kernel, n, c),
            [mine, across(mine, 1)],
            free=[shaped((5 * c, chans), BF16), shaped((2, wide), F32), shaped((n, 2 * c), F32)],
            name="kernel_grad",
        )
    else:
        core = lax.axis_index("dp") % 2
        both = jnp.stack([keep, send.astype(F32)])
        both = jnp.where(core == 0, both, both[::-1]).transpose(1, 2, 0, 3).reshape(5 * c, chans)
        both, gains = lax.psum((both, gains), "dp")
        taps_grad, gains = (both * scale).astype(BF16), gains * scale
        whalf = gate(whalf, gains)
        within = lambda v: pltpu.with_memory_space_constraint(v, pltpu.VMEM)
        weight_grad = pl.pallas_call(
            weave_kernel,
            out_shape=pltpu.HBM((chips, 2, width // m, cols), BF16),
            in_specs=[VMEM, VMEM],
            out_specs=HBM,
            scratch_shapes=[pltpu.SemaphoreType.DMA((m,))],
            compiler_params=pltpu.CompilerParams(vmem_limit_bytes=SPARE << 20),
            cost_estimate=pl.CostEstimate(flops=0, bytes_accessed=0, transcendentals=0),
            name="weight_grad",
        )(within(whalf), within(across(whalf, 1)))
        gain_in_grad = jnp.sum(gains[:, : chans // 128], axis=0)
        gain_mid_grad = gains[:, chans // 128 :].reshape(n, -1)[:, : 2 * c]
    return (
        qkv[None],
        input_grad.reshape(1, length, chans),
        taps_grad.reshape(5, c, chans).transpose(0, 2, 1),
        gain_in_grad.reshape(chans),
        gain_mid_grad.reshape(n, 2, c).transpose(1, 0, 2).reshape(width),
        weight_grad.reshape(width, cols),
    )


def solution(mesh):
    placed = (
        P("dp", "seq", None),
        P(None, None, "seq"),
        P(None, "seq"),
        P(),
        P(),
        P("dp", None, "seq"),
    )
    return jax.shard_map(
        body,
        mesh=mesh,
        in_specs=placed,
        out_specs=(
            P("dp", None, "seq"),
            P("dp", "seq", None),
            P(None, None, "seq"),
            P(),
            P(),
            P(None, "seq"),
        ),
        check_vma=False,
    )
```

```python
import functools
import math

import jax
import jax.numpy as jnp
from jax import lax
from jax.experimental import pallas as pl
from jax.experimental.pallas import tpu as pltpu
from jax.sharding import PartitionSpec as P

EPS = 1e-06
WAIT = 4e10
SPARE = 12
F32 = jnp.float32
BF16 = jnp.bfloat16
ANY = pl.BlockSpec(memory_space=pl.ANY)
HBM = pl.BlockSpec(memory_space=pltpu.HBM)
VMEM = pl.BlockSpec(memory_space=pltpu.VMEM)


class In:
    def __init__(self, ref, copy=None):
        self.ref, self.copy = ref, copy
        if copy is not None:
            copy.start()

    def __call__(self):
        if self.copy is not None:
            self.copy.wait()
            self.copy = None
        return self.ref


def shaped(shape, dtype):
    return jax.ShapeDtypeStruct(shape, dtype)


class Far:
    def __init__(self, value):
        self.value = value


def call(kernel, args, outs=(), free=(), kept=(), after=(), near=(), spill=(), fetch=(), scratch=(), flops=0, name=None):
    within = lambda v: pltpu.with_memory_space_constraint(v, pltpu.VMEM)
    near, spill = [within(v) for v in near], [within(v) for v in spill]
    fetch = [pltpu.with_memory_space_constraint(v, pltpu.HBM) for v in fetch]
    after = [pltpu.with_memory_space_constraint(v, pltpu.HBM) for v in after]
    far = [i for i, v in enumerate(args) if isinstance(v, Far)]
    args = [pltpu.with_memory_space_constraint(v.value, pltpu.HBM) if isinstance(v, Far) else v for v in args]
    count, skip = len(args), len(after) + len(near)
    lanes = lambda v: math.prod(v.shape[:-1]) * -(-v.shape[-1] // 128) * 128 * v.dtype.itemsize
    need = sum(map(lanes, [*args, *outs, *free, *scratch]))

    def whole(*refs):
        refs = list(refs)
        take = lambda k: [refs.pop(0) for _ in range(k)]
        ins, _, saved, fetched = take(count), take(skip), take(len(spill)), take(len(fetch))
        targets, rest, places, nears = take(len(outs)), take(len(free) + len(kept)), take(len(spill)), take(len(fetch))
        own, landed, made = take(len(scratch)), take(len(far)), take(len(outs))
        in_sems, out_sems = refs
        operands = [In(v) for v in ins]
        for k, i in enumerate(far):
            operands[i] = In(landed[k], pltpu.make_async_copy(ins[i], landed[k], in_sems.at[k]))
        pairs = [*zip(made, targets), *zip(saved, places), *zip(fetched, nears)]
        copies = [pltpu.make_async_copy(v, t, out_sems.at[k]) for k, (v, t) in enumerate(pairs)]
        operands += [In(t, copy) for t, copy in zip(nears, copies[len(pairs) - len(nears) :])]
        copies = copies[: len(pairs) - len(nears)]
        gone = [False] * len(made)

        def go(ref):
            k = next(i for i, v in enumerate(made) if v is ref)
            gone[k] = True
            copies[k].start()

        for copy in copies[len(made) :]:
            copy.start()
        kernel(operands, [*made, *rest], go, *own)
        for k, copy in enumerate(copies[: len(made)]):
            if not gone[k]:
                copy.start()
        for v in operands:
            v()
        for copy in copies:
            copy.wait()

    specs = [VMEM] * count
    for i in far:
        specs[i] = HBM
    memory = lambda space, values: [space(v.shape, v.dtype) for v in values]
    return pl.pallas_call(
        whole,
        out_shape=tuple(
            [*memory(pltpu.HBM, outs), *free, *memory(pltpu.VMEM, kept), *memory(pltpu.HBM, spill)]
            + memory(pltpu.VMEM, fetch)
        ),
        in_specs=specs + [HBM] * len(after) + [VMEM] * (len(near) + len(spill)) + [HBM] * len(fetch),
        out_specs=tuple([HBM] * len(outs) + [VMEM] * (len(free) + len(kept)) + [HBM] * len(spill) + [VMEM] * len(fetch)),
        scratch_shapes=[
            *scratch,
            *memory(pltpu.VMEM, [args[i] for i in far]),
            *memory(pltpu.VMEM, outs),
            pltpu.SemaphoreType.DMA((max(1, len(far)),)),
            pltpu.SemaphoreType.DMA((max(1, len(outs) + len(spill) + len(fetch)),)),
        ],
        compiler_params=pltpu.CompilerParams(vmem_limit_bytes=min(56 << 20, need + (SPARE << 20))),
        cost_estimate=pl.CostEstimate(flops=int(flops), bytes_accessed=0, transcendentals=0),
        name=name,
    )(*args, *after, *near, *spill, *fetch)


def gate(value, after, space=pltpu.VMEM):
    spec = pl.BlockSpec(memory_space=space)
    return pl.pallas_call(
        lambda *_: None,
        out_shape=space(value.shape, value.dtype),
        in_specs=[spec, ANY],
        out_specs=spec,
        input_output_aliases={0: 0},
        compiler_params=pltpu.CompilerParams(vmem_limit_bytes=SPARE << 20),
        cost_estimate=pl.CostEstimate(flops=0, bytes_accessed=0, transcendentals=0),
        name="gate",
    )(pltpu.with_memory_space_constraint(value, space), after)


def dot(a, b):
    return jnp.dot(a, b, preferred_element_type=F32)


def dot_nt(a, b):
    return lax.dot_general(a, b, (((1,), (1,)), ((), ())), preferred_element_type=F32)


def dot_tn(a, b):
    return lax.dot_general(a, b, (((0,), (0,)), ((), ())), preferred_element_type=F32)


def later(v):
    row = lax.broadcasted_iota(jnp.int32, v.shape, 0)
    return jnp.where(row == 0, 0.0, pltpu.roll(v, 1, 0))


def sooner(v):
    rows = v.shape[0]
    row = lax.broadcasted_iota(jnp.int32, v.shape, 0)
    return jnp.where(row == rows - 1, 0.0, pltpu.roll(v, rows - 1, 0))


def inv_rms(v):
    return lax.rsqrt(jnp.mean(v * v, axis=-1, keepdims=True) + EPS)


def in_two(v):
    high = v.astype(BF16).astype(F32)
    return jnp.concatenate([high, v - high], axis=0).astype(BF16)


def joined(tail):
    rows = tail.shape[0] // 2
    return tail[:rows].astype(F32) + tail[rows:].astype(F32)


def picker(shape, me, c):
    row = lax.broadcasted_iota(jnp.int32, shape, 0)
    col = lax.broadcasted_iota(jnp.int32, shape, 1)
    return jnp.where(row == col + me * c, 1.0, 0.0).astype(BF16)


def mid_kernel(n, c, chans, ins, outs, go):
    me = lax.axis_index("seq")
    cot, w = ins[:2]
    g, w = cot()[...], w()
    for k in range(n):
        at = pl.multiple_of(lax.rem(me + k, n) * c, c & -c)
        rows = jnp.concatenate([w[pl.ds(at, c), :], w[pl.ds(chans + at, c), :]], axis=0)
        outs[k][...] = dot_nt(g, rows).astype(BF16)


def conv_kernel_fwd(n, c, chans, ins, outs, go, xs):
    me = lax.axis_index("seq")
    blocks, (taps, gain) = ins[:n], ins[n:]
    pooled_msg, pooled, conv_out, nin, rone = outs
    rows = blocks[0].ref.shape[0]
    gains = gain()[...]
    for k in range(n):
        at = pl.multiple_of(lax.rem(me - k + n, n) * rows, rows)
        v = blocks[k]()[...]
        xs[pl.ds(at, rows), :] = v
        for h in range(2):
            f = v[:, h * chans : (h + 1) * chans].astype(F32)
            r = inv_rms(f)
            rone[pl.ds(at, rows), h : h + 1] = r
            nin[pl.ds(at, rows), h * chans : (h + 1) * chans] = (f * r * gains).astype(BF16)
    nin = nin
    xe, xo = nin[:, :chans], nin[:, chans:]
    taps = taps()
    k0, k1, k2, k3, k4 = (taps[k * c : (k + 1) * c, :] for k in range(5))
    even = dot_nt(xe, k2) + dot_nt(xo, k3) + later(dot_nt(xe, k0) + dot_nt(xo, k1)) + sooner(dot_nt(xe, k4))
    odd = dot_nt(xe, k1) + dot_nt(xo, k2) + later(dot_nt(xo, k0)) + sooner(dot_nt(xe, k3) + dot_nt(xo, k4))
    conv = jnp.concatenate([even, odd], axis=1)
    pick = picker((chans, c), me, c)
    own = jnp.concatenate([dot(xs[:, :chans], pick), dot(xs[:, chans:], pick)], axis=1)
    total = own + conv * jax.nn.sigmoid(conv)
    pooled_msg[...] = total.astype(BF16)
    conv_out[...] = conv
    pooled[...] = total


def qkv_kernel(n, c, chans, ins, outs, go):
    me = lax.axis_index("seq")
    blocks, mids = ins[:n], ins[n : 2 * n]
    gains, cot, w = ins[2 * n :]
    nmt, rtwo, qkv, part, *msgs = outs
    squares = 0.0
    for v in blocks:
        v = v()[...].astype(F32)
        squares = squares + jnp.sum(v * v, axis=1, keepdims=True)
    r = lax.rsqrt(squares * (1.0 / (2 * chans)) + EPS)
    rtwo[...] = r
    gains = gains()
    for k in range(n):
        b = lax.rem(me - k + n, n)
        v = blocks[k]()[...].astype(F32) * r * gains[pl.ds(b, 1), :]
        t = v.T.astype(BF16)
        for h in range(2):
            at = pl.multiple_of(h * chans + b * c, c & -c)
            nmt[pl.ds(at, c), :] = t[h * c : (h + 1) * c, :]
    go(nmt)
    half, wide = mids[0].ref.shape
    q = dot_tn(nmt[...], w()[...])
    qkv[...] = q.astype(BF16)
    go(qkv)
    row = jnp.sum(q * cot()[...].astype(F32), axis=1, keepdims=True)
    row = jnp.broadcast_to(row, (row.shape[0], 128)).T[:8, :]
    part[...] = row
    if msgs:
        if half < wide:
            row = jnp.concatenate([row, jnp.zeros((8, wide - half), F32)], axis=1)
        for k in range(n):
            msgs[k][:half, :] = mids[k]()[...]
            msgs[k][half:, :] = in_two(row)
            go(msgs[k])


def back_kernel(n, c, chans, m, ins, outs, go, evens, odds, whole, spare):
    seq_at = lax.axis_index("seq")
    core = lax.rem(lax.axis_index("dp"), 2)
    mids, parts = ins[:n], ins[n:-8]
    pooled, rtwo, conv_out, gmid, nin, gin, rone, taps = ins[-8:]
    send, keep, *msgs = outs
    half = rtwo().shape[0]
    r = rtwo()[...]
    atwo = pooled()[...] * r
    conv = conv_out()[...]
    sig = jax.nn.sigmoid(conv)
    slope = sig * (1.0 + conv * (1.0 - sig))
    gains = gmid()[pl.ds(seq_at, 1), :]
    mid, rowsum = 0.0, 0.0
    for v in mids:
        mid = mid + v()[:half, :].astype(F32)
    if parts:
        for v in parts:
            rowsum = rowsum + v()[...]
    else:
        for v in mids:
            rowsum = rowsum + joined(v()[half:, :])[:, :half]
    mean = jnp.concatenate([rowsum] * 16, axis=0).T[:, :1] * (1.0 / (2 * chans))
    section = r * (gains * mid - atwo * mean)
    cg = section * slope
    cg = cg.astype(BF16).astype(F32)
    ge, gd = cg[:, :c], cg[:, c:]
    bf = lambda v: v.astype(BF16)
    g0, gp, gm = bf(ge), bf(sooner(ge)), bf(later(ge))
    o0, op, om = bf(gd), bf(sooner(gd)), bf(later(gd))
    evens[...] = jnp.concatenate((gp, o0, g0, om, gm), axis=1)
    odds[...] = jnp.concatenate((op, gp, o0, g0, om), axis=1)
    wide, rows = chans // 2, 5 * c // (m // 2)
    nin = nin()
    for out, which in ((send, 1 - core), (keep, core)):
        at = pl.multiple_of(which * wide, wide & -wide)
        kg = dot_tn(evens[...], nin[:, pl.ds(at, wide)]) + dot_tn(odds[...], nin[:, pl.ds(chans + at, wide)])
        for q in range(m // 2):
            out[q] = kg[q * rows : (q + 1) * rows, :].astype(out.dtype)
        go(out)
    width = 2 * chans
    block = half // n
    gin, rone, taps = gin()[...], rone()[...], taps()[...]
    pick = picker((chans, c), seq_at, c)
    grad = section.astype(BF16)
    acc = 0.0
    lane = lax.broadcasted_iota(jnp.int32, (half, 128), 1)
    means = jnp.zeros((half, 128), F32)
    for h, g in ((0, evens), (1, odds)):
        ng = dot(g[...], taps)
        aone = nin[:, h * chans : (h + 1) * chans].astype(F32) / gin
        acc = acc + jnp.sum(ng * aone, axis=0, keepdims=True)
        placed = dot_nt(grad[:, h * c : (h + 1) * c], pick)
        means = jnp.where(lane == h, jnp.mean(placed * aone, axis=1, keepdims=True), means)
        total = (placed + rone[:, h : h + 1] * gin * ng).astype(BF16)
        whole[:, h * chans : (h + 1) * chans] = total
    spare[...] = means
    mid = jnp.sum(mid * atwo, axis=0, keepdims=True)
    short = -2 * c % 128
    if short:
        mid = jnp.concatenate([mid, jnp.zeros((1, short), F32)], axis=1)
    line = lax.broadcasted_iota(jnp.int32, (16, 128), 0)
    gains = jnp.zeros((16, 128), F32)
    vector = jnp.concatenate([acc, mid], axis=1)
    for i in range(vector.shape[1] // 128):
        gains = jnp.where(line == i, vector[:, i * 128 : (i + 1) * 128], gains)
    gains = in_two(gains)
    for k in range(n):
        at = pl.multiple_of(lax.rem(seq_at + k, n) * block, block)
        msgs[k][:, :width] = whole[pl.ds(at, block), :]
        msgs[k][:, width:] = jnp.zeros((block, 128), BF16)
        msgs[k][:32, width:] = gains
        mean = spare[pl.ds(at, block), :].T[:16, :]
        msgs[k][32:48, width : width + block] = mean.astype(BF16)
        go(msgs[k])


def weight_kernel(m, scale, ins, outs, go):
    core = lax.rem(lax.axis_index("dp"), 2)
    nms, total = ins[0](), 0.0
    for v, which in zip(ins[1:], (core, 1 - core)):
        v = v()
        for q in range(m // 2):
            total = total + dot(nms[2 * q + which], v[q])
    total = (total * scale).astype(BF16)
    for q in range(m // 2):
        outs[0][q] = total


def split_kernel(q, ins, outs, go):
    keep, recv = ins
    me = lax.axis_index("dp") // 2
    keep, recv = keep(), recv()
    for k in [*range(1, q), 0]:
        out = outs[k - 1]
        out[...] = (keep[me ^ k] + recv[me ^ k].astype(F32)).astype(out.dtype)


def finish_kernel(n, chans, scale, ins, outs, go):
    total = ins[0]()[...]
    for r in ins[1:-1]:
        total = total + r()[...].astype(F32)
    rows, wide = total.shape
    outs[0][:rows, :] = (total * scale).astype(BF16)
    gains = ins[-1]()
    pieces, count = wide // 128, chans // 128
    both = gains[0]
    for b in range(1, n):
        both = both + gains[b]
    line = lax.broadcasted_iota(jnp.int32, (8, wide), 0)
    tail = jnp.zeros((8, wide), F32)
    wanted = [(i, both, i * pieces) for i in range(2)] + [(2 + b, gains[b], count) for b in range(n)]
    for i, source, first in wanted:
        row = jnp.concatenate([source[first + j : first + j + 1, :] for j in range(pieces)], axis=1)
        tail = jnp.where(line == i, row, tail)
    outs[0][rows:, :] = in_two(tail * scale)


def half_kernel(q, ins, outs, go):
    me = lax.axis_index("dp") // 2
    out = outs[0]
    rows = ins[0].ref.shape[0] - 16
    tail = 0.0
    for k in range(q):
        at = pl.multiple_of((me ^ k) * rows, rows & -rows)
        out[pl.ds(at, rows), :] = ins[k]()[:rows, :]
        tail = tail + joined(ins[k]()[rows:, :])
    out[q * rows :, :] = in_two(tail)


def place_kernel(n, c, ins, outs, go):
    core = lax.rem(lax.axis_index("dp"), 2)
    mine, other = ins
    taps, gain_in, gain_mid = outs
    rows, wide = taps.shape[0], mine.ref.shape[1]
    total = 0.0
    for v, which in ((mine, core), (other, 1 - core)):
        side = pl.multiple_of(which * wide, wide & -wide)
        taps[:, pl.ds(side, wide)] = v()[:rows, :]
        total = total + joined(v()[rows:, :])
    gain_in[...] = jnp.concatenate([total[0:1, :], total[1:2, :]], axis=1).reshape(gain_in.shape)
    pieces = [total[2 + b : 3 + b, h * c : (h + 1) * c] for h in range(2) for b in range(n)]
    gain_mid[...] = jnp.concatenate(pieces, axis=1).reshape(gain_mid.shape)


def weave_kernel(mine, other, *refs):
    core = lax.rem(lax.axis_index("dp"), 2)
    out, sems = refs[-2:]
    copies = []
    for v, which in ((mine, core), (other, 1 - core)):
        for q in range(v.shape[0]):
            copies.append(pltpu.make_async_copy(v.at[q], out.at[q, which], sems.at[len(copies)]))
    for copy in copies:
        copy.start()
    for copy in copies:
        copy.wait()


def input_kernel(n, chans, ins, outs, go):
    me = lax.axis_index("seq")
    got, own = ins[:n], ins[n]
    out, gains = outs
    total = got[0]()[...].astype(F32)
    for v in got[1:]:
        total = total + v()[...].astype(F32)
    for k in range(n):
        gains[lax.rem(me - k + n, n)] = joined(got[k]()[:32, 2 * chans :])
    rows = total.shape[0]
    means = jnp.concatenate([total[32:48, 2 * chans :]] * 8, axis=0).T
    for h in range(2):
        x = own()[:, h * chans : (h + 1) * chans].astype(F32)
        a = x * inv_rms(x)
        t = total[:, h * chans : (h + 1) * chans]
        mean = means[:rows, h : h + 1]
        v = t - a * (jnp.mean(t * a, axis=-1, keepdims=True) - mean)
        out[:, h * chans : (h + 1) * chans] = v.astype(BF16)


def body(section_input, conv_kernel, qkv_weight, gain_in, gain_mid, qkv_cotangent):
    x = section_input[0]
    cot = qkv_cotangent[0]
    length, chans = x.shape
    c = conv_kernel.shape[2]
    width, cols = qkv_weight.shape
    n, m = lax.axis_size("seq"), lax.axis_size("dp")
    half = length // 2 * n
    scale = 1.0 / math.sqrt(m * half)
    shift = lambda v, k: lax.ppermute(v, "seq", [(i, (i + k) % n) for i in range(n)])
    from_all = lambda v: [v] + [shift(v, k) for k in range(1, n)]
    across = lambda v, k: lax.ppermute(v, "dp", [(i, i ^ k) for i in range(m)])
    same_core = [[i for i in range(m) if i % 2 == core] for core in range(2)]
    chips = m // 2
    rows, wide = 5 * c // chips, chans // 2

    taps_rows = conv_kernel.transpose(0, 2, 1).reshape(5 * c, chans)
    own = x.reshape(length // 2, width)
    xs = from_all(own)
    gin = gain_in.reshape(1, chans)
    gmid = gain_mid.reshape(2, n, c).transpose(1, 0, 2).reshape(n, 2 * c)
    cots = jnp.broadcast_to(cot[None], (chips, *cot.shape))
    cots = lax.all_to_all(cots, "dp", 0, 0, axis_index_groups=same_core, tiled=True)
    used = [cot, qkv_weight, taps_rows, gin, gmid]
    held = call(
        functools.partial(mid_kernel, n, c, chans),
        [],
        kept=[shaped((half, 2 * c), BF16)] * n,
        fetch=used,
        flops=WAIT,
        name="mid_parts",
    )
    mid_msgs = held[:n]
    cot, weight, taps, gin, gmid = held[n:]
    pooled_msg, *states = call(
        functools.partial(conv_kernel_fwd, n, c, chans),
        [*xs, taps, gin],
        free=[shaped((half, 2 * c), BF16)],
        kept=[
            shaped((half, 2 * c), F32),
            shaped((half, 2 * c), F32),
            shaped((half, width), BF16),
            shaped((half, 2), F32),
        ],
        scratch=[pltpu.VMEM((half, width), BF16)],
        name="conv_forward",
    )
    blocks = from_all(pooled_msg)
    rides = half <= 2 * c
    nmt, rtwo, qkv, part, *tailed, pooled, conv_out, nin, rone = call(
        functools.partial(qkv_kernel, n, c, chans),
        [*blocks, *mid_msgs, gmid, cot, weight],
        outs=[
            shaped((width, half), BF16),
            shaped((half, 1), F32),
            shaped((half, cols), BF16),
            shaped((8, half), F32),
        ]
        + [shaped((half + 16, 2 * c), BF16)] * (n * rides),
        spill=states,
        name="qkv",
    )
    cots = gate(cots, nmt, pltpu.HBM)
    mid_msgs = tailed if rides else mid_msgs
    mids = [mid_msgs[0]] + [shift(mid_msgs[k], k) for k in range(1, n)]
    parts = [] if rides else from_all(part)
    nms = lax.all_to_all(nmt.reshape(m, width // m, half), "dp", 0, 0, tiled=True)
    (wshare,) = call(
        functools.partial(weight_kernel, m, scale),
        [nms, Far(cots), Far(across(cots, 1))],
        outs=[shaped((chips, width // m, cols), BF16)],
        name="weight_share",
    )
    whalf = lax.all_to_all(wshare, "dp", 0, 0, axis_index_groups=same_core, tiled=True)
    send, keep, *msgs = call(
        functools.partial(back_kernel, n, c, chans, m),
        [
            Far(mids[0]),
            *mids[1:],
            *parts,
            *map(Far, [pooled, rtwo, conv_out]),
            gmid,
            Far(nin),
            gin,
            Far(rone),
            Far(taps_rows),
        ],
        outs=[
            shaped((chips, rows, wide), BF16),
            shaped((chips, rows, wide), F32),
        ]
        + [shaped((half // n, width + 128), BF16)] * n,
        scratch=[
            pltpu.VMEM((half, 5 * c), BF16),
            pltpu.VMEM((half, 5 * c), BF16),
            pltpu.VMEM((half, width), BF16),
            pltpu.VMEM((half, 128), F32),
        ],
        after=[wshare],
        flops=WAIT,
        name="conv_backward",
    )
    got = [msgs[0]] + [shift(msgs[k], k) for k in range(1, n)]
    input_grad, gains = call(
        functools.partial(input_kernel, n, chans),
        [*got, own],
        free=[shaped((length // 2, width), BF16), shaped((n, 16, 128), F32)],
        name="input_grad",
    )
    *split, keep_sum = call(
        functools.partial(split_kernel, chips),
        [Far(keep), across(send, 1)],
        free=[shaped((rows, wide), BF16)] * (chips - 1),
        kept=[shaped((rows, wide), F32)],
        name="core_sum",
    )
    if rows % 16 == 0 and n <= 6:
        (kshare,) = call(
            functools.partial(finish_kernel, n, chans, scale),
            [keep_sum] + [across(split[k - 1], 2 * k) for k in range(1, chips)] + [gains],
            free=[shaped((rows + 16, wide), BF16)],
            name="chip_sum",
        )
        whalf = gate(whalf, kshare)
        within = lambda v: pltpu.with_memory_space_constraint(v, pltpu.VMEM)
        weight_grad = pl.pallas_call(
            weave_kernel,
            out_shape=pltpu.HBM((chips, 2, width // m, cols), BF16),
            in_specs=[VMEM, VMEM],
            out_specs=HBM,
            scratch_shapes=[pltpu.SemaphoreType.DMA((m,))],
            compiler_params=pltpu.CompilerParams(vmem_limit_bytes=SPARE << 20),
            cost_estimate=pl.CostEstimate(flops=0, bytes_accessed=0, transcendentals=0),
            name="weight_grad",
        )(within(whalf), within(across(whalf, 1)))
        kshares = [kshare] + [across(kshare, k) for k in range(2, m, 2)]
        (mine,) = call(
            functools.partial(half_kernel, chips),
            kshares,
            free=[shaped((5 * c + 16, wide), BF16)],
            after=[weight_grad],
            name="kernel_grad_half",
        )
        taps_grad, gain_in_grad, gain_mid_grad = call(
            functools.partial(place_kernel, n, c),
            [mine, across(mine, 1)],
            free=[shaped((5 * c, chans), BF16), shaped((chans,), F32), shaped((width,), F32)],
            name="kernel_grad",
        )
    else:
        core = lax.axis_index("dp") % 2
        both = jnp.stack([keep, send.astype(F32)])
        both = jnp.where(core == 0, both, both[::-1]).transpose(1, 2, 0, 3).reshape(5 * c, chans)
        both, gains = lax.psum((both, gains), "dp")
        taps_grad, gains = (both * scale).astype(BF16), gains * scale
        whalf = gate(whalf, gains)
        within = lambda v: pltpu.with_memory_space_constraint(v, pltpu.VMEM)
        weight_grad = pl.pallas_call(
            weave_kernel,
            out_shape=pltpu.HBM((chips, 2, width // m, cols), BF16),
            in_specs=[VMEM, VMEM],
            out_specs=HBM,
            scratch_shapes=[pltpu.SemaphoreType.DMA((m,))],
            compiler_params=pltpu.CompilerParams(vmem_limit_bytes=SPARE << 20),
            cost_estimate=pl.CostEstimate(flops=0, bytes_accessed=0, transcendentals=0),
            name="weight_grad",
        )(within(whalf), within(across(whalf, 1)))
        gain_in_grad = jnp.sum(gains[:, : chans // 128], axis=0)
        gain_mid_grad = gains[:, chans // 128 :].reshape(n, -1)[:, : 2 * c]
        gain_mid_grad = gain_mid_grad.reshape(n, 2, c).transpose(1, 0, 2)
    return (
        qkv[None],
        input_grad.reshape(1, length, chans),
        taps_grad.reshape(5, c, chans).transpose(0, 2, 1),
        gain_in_grad.reshape(chans),
        gain_mid_grad.reshape(width),
        weight_grad.reshape(width, cols),
    )


def solution(mesh):
    placed = (
        P("dp", "seq", None),
        P(None, None, "seq"),
        P(None, "seq"),
        P(),
        P(),
        P("dp", None, "seq"),
    )
    return jax.shard_map(
        body,
        mesh=mesh,
        in_specs=placed,
        out_specs=(
            P("dp", None, "seq"),
            P("dp", "seq", None),
            P(None, None, "seq"),
            P(),
            P(),
            P(None, "seq"),
        ),
        check_vma=False,
    )
```

```python
import functools
import math

import jax
import jax.numpy as jnp
from jax import lax
from jax.experimental import pallas as pl
from jax.experimental.pallas import tpu as pltpu
from jax.sharding import PartitionSpec as P

EPS = 1e-06
WAIT = 4e10
SPARE = 12
F32 = jnp.float32
BF16 = jnp.bfloat16
ANY = pl.BlockSpec(memory_space=pl.ANY)
HBM = pl.BlockSpec(memory_space=pltpu.HBM)
VMEM = pl.BlockSpec(memory_space=pltpu.VMEM)


class In:
    def __init__(self, ref, copy=None):
        self.ref, self.copy = ref, copy
        if copy is not None:
            copy.start()

    def __call__(self):
        if self.copy is not None:
            self.copy.wait()
            self.copy = None
        return self.ref


def shaped(shape, dtype):
    return jax.ShapeDtypeStruct(shape, dtype)


class Far:
    def __init__(self, value):
        self.value = value


def call(kernel, args, outs=(), free=(), kept=(), after=(), near=(), spill=(), fetch=(), scratch=(), flops=0, name=None):
    within = lambda v: pltpu.with_memory_space_constraint(v, pltpu.VMEM)
    near, spill = [within(v) for v in near], [within(v) for v in spill]
    fetch = [pltpu.with_memory_space_constraint(v, pltpu.HBM) for v in fetch]
    after = [pltpu.with_memory_space_constraint(v, pltpu.HBM) for v in after]
    far = [i for i, v in enumerate(args) if isinstance(v, Far)]
    args = [pltpu.with_memory_space_constraint(v.value, pltpu.HBM) if isinstance(v, Far) else v for v in args]
    count, skip = len(args), len(after) + len(near)
    lanes = lambda v: math.prod(v.shape[:-1]) * -(-v.shape[-1] // 128) * 128 * v.dtype.itemsize
    need = sum(map(lanes, [*args, *outs, *free, *scratch]))

    def whole(*refs):
        refs = list(refs)
        take = lambda k: [refs.pop(0) for _ in range(k)]
        ins, _, saved, fetched = take(count), take(skip), take(len(spill)), take(len(fetch))
        targets, rest, places, nears = take(len(outs)), take(len(free) + len(kept)), take(len(spill)), take(len(fetch))
        own, landed, made = take(len(scratch)), take(len(far)), take(len(outs))
        in_sems, out_sems = refs
        operands = [In(v) for v in ins]
        for k, i in enumerate(far):
            operands[i] = In(landed[k], pltpu.make_async_copy(ins[i], landed[k], in_sems.at[k]))
        pairs = [*zip(made, targets), *zip(saved, places), *zip(fetched, nears)]
        copies = [pltpu.make_async_copy(v, t, out_sems.at[k]) for k, (v, t) in enumerate(pairs)]
        operands += [In(t, copy) for t, copy in zip(nears, copies[len(pairs) - len(nears) :])]
        copies = copies[: len(pairs) - len(nears)]
        gone = [False] * len(made)

        def go(ref):
            k = next(i for i, v in enumerate(made) if v is ref)
            gone[k] = True
            copies[k].start()

        for copy in copies[len(made) :]:
            copy.start()
        kernel(operands, [*made, *rest], go, *own)
        for k, copy in enumerate(copies[: len(made)]):
            if not gone[k]:
                copy.start()
        for v in operands:
            v()
        for copy in copies:
            copy.wait()

    specs = [VMEM] * count
    for i in far:
        specs[i] = HBM
    memory = lambda space, values: [space(v.shape, v.dtype) for v in values]
    return pl.pallas_call(
        whole,
        out_shape=tuple(
            [*memory(pltpu.HBM, outs), *free, *memory(pltpu.VMEM, kept), *memory(pltpu.HBM, spill)]
            + memory(pltpu.VMEM, fetch)
        ),
        in_specs=specs + [HBM] * len(after) + [VMEM] * (len(near) + len(spill)) + [HBM] * len(fetch),
        out_specs=tuple([HBM] * len(outs) + [VMEM] * (len(free) + len(kept)) + [HBM] * len(spill) + [VMEM] * len(fetch)),
        scratch_shapes=[
            *scratch,
            *memory(pltpu.VMEM, [args[i] for i in far]),
            *memory(pltpu.VMEM, outs),
            pltpu.SemaphoreType.DMA((max(1, len(far)),)),
            pltpu.SemaphoreType.DMA((max(1, len(outs) + len(spill) + len(fetch)),)),
        ],
        compiler_params=pltpu.CompilerParams(vmem_limit_bytes=min(56 << 20, need + (SPARE << 20))),
        cost_estimate=pl.CostEstimate(flops=int(flops), bytes_accessed=0, transcendentals=0),
        name=name,
    )(*args, *after, *near, *spill, *fetch)


def gate(value, after, space=pltpu.VMEM):
    spec = pl.BlockSpec(memory_space=space)
    return pl.pallas_call(
        lambda *_: None,
        out_shape=space(value.shape, value.dtype),
        in_specs=[spec, ANY],
        out_specs=spec,
        input_output_aliases={0: 0},
        compiler_params=pltpu.CompilerParams(vmem_limit_bytes=SPARE << 20),
        cost_estimate=pl.CostEstimate(flops=0, bytes_accessed=0, transcendentals=0),
        name="gate",
    )(pltpu.with_memory_space_constraint(value, space), after)


def dot(a, b):
    return jnp.dot(a, b, preferred_element_type=F32)


def dot_nt(a, b):
    return lax.dot_general(a, b, (((1,), (1,)), ((), ())), preferred_element_type=F32)


def dot_tn(a, b):
    return lax.dot_general(a, b, (((0,), (0,)), ((), ())), preferred_element_type=F32)


def later(v):
    row = lax.broadcasted_iota(jnp.int32, v.shape, 0)
    return jnp.where(row == 0, 0.0, pltpu.roll(v, 1, 0))


def sooner(v):
    rows = v.shape[0]
    row = lax.broadcasted_iota(jnp.int32, v.shape, 0)
    return jnp.where(row == rows - 1, 0.0, pltpu.roll(v, rows - 1, 0))


def inv_rms(v):
    return lax.rsqrt(jnp.mean(v * v, axis=-1, keepdims=True) + EPS)


def in_two(v):
    high = v.astype(BF16).astype(F32)
    return jnp.concatenate([high, v - high], axis=0).astype(BF16)


def joined(tail):
    rows, tail = tail.shape[0] // 2, tail.astype(F32)
    return tail[:rows] + tail[rows:]


def picker(shape, me, c):
    row = lax.broadcasted_iota(jnp.int32, shape, 0)
    col = lax.broadcasted_iota(jnp.int32, shape, 1)
    return jnp.where(row == col + me * c, 1.0, 0.0).astype(BF16)


def mid_kernel(n, c, chans, ins, outs, go):
    me = lax.axis_index("seq")
    gain_in, gain_mid, cot, w = ins[:4]
    gin, gmid = outs[n:]
    gin[...] = gain_in()[...].reshape(1, chans)
    gains = gain_mid()[...].reshape(1, 2 * chans)
    for b in range(n):
        pair = [gains[:, h * chans + b * c : h * chans + (b + 1) * c] for h in range(2)]
        gmid[b : b + 1, :] = jnp.concatenate(pair, axis=1)
    g, w = cot()[...], w()
    for k in range(n):
        at = pl.multiple_of(lax.rem(me + k, n) * c, c & -c)
        rows = jnp.concatenate([w[pl.ds(at, c), :], w[pl.ds(chans + at, c), :]], axis=0)
        outs[k][...] = dot_nt(g, rows).astype(BF16)


def conv_kernel_fwd(n, c, chans, ins, outs, go, xs):
    me = lax.axis_index("seq")
    blocks, (taps, gain) = ins[:n], ins[n:]
    pooled_msg, pooled, conv_out, nin, rone = outs
    rows = blocks[0].ref.shape[0]
    gains = gain()[...]
    for k in range(n):
        at = pl.multiple_of(lax.rem(me - k + n, n) * rows, rows)
        v = blocks[k]()[...]
        xs[pl.ds(at, rows), :] = v
        for h in range(2):
            f = v[:, h * chans : (h + 1) * chans].astype(F32)
            r = inv_rms(f)
            rone[pl.ds(at, rows), h : h + 1] = r
            nin[pl.ds(at, rows), h * chans : (h + 1) * chans] = (f * r * gains).astype(BF16)
    nin = nin
    xe, xo = nin[:, :chans], nin[:, chans:]
    taps = taps()
    k0, k1, k2, k3, k4 = (taps[k * c : (k + 1) * c, :] for k in range(5))
    even = dot_nt(xe, k2) + dot_nt(xo, k3) + later(dot_nt(xe, k0) + dot_nt(xo, k1)) + sooner(dot_nt(xe, k4))
    odd = dot_nt(xe, k1) + dot_nt(xo, k2) + later(dot_nt(xo, k0)) + sooner(dot_nt(xe, k3) + dot_nt(xo, k4))
    conv = jnp.concatenate([even, odd], axis=1)
    pick = picker((chans, c), me, c)
    own = jnp.concatenate([dot(xs[:, :chans], pick), dot(xs[:, chans:], pick)], axis=1)
    total = own + conv * jax.nn.sigmoid(conv)
    pooled_msg[...] = total.astype(BF16)
    conv_out[...] = conv
    pooled[...] = total


def qkv_kernel(n, c, chans, ins, outs, go):
    me = lax.axis_index("seq")
    blocks, mids = ins[:n], ins[n : 2 * n]
    gains, cot, w = ins[2 * n :]
    nmt, rtwo, qkv, part, *msgs = outs
    squares = 0.0
    for v in blocks:
        v = v()[...].astype(F32)
        squares = squares + jnp.sum(v * v, axis=1, keepdims=True)
    r = lax.rsqrt(squares * (1.0 / (2 * chans)) + EPS)
    rtwo[...] = r
    gains = gains()
    for k in range(n):
        b = lax.rem(me - k + n, n)
        v = blocks[k]()[...].astype(F32) * r * gains[pl.ds(b, 1), :]
        t = v.T.astype(BF16)
        for h in range(2):
            at = pl.multiple_of(h * chans + b * c, c & -c)
            nmt[pl.ds(at, c), :] = t[h * c : (h + 1) * c, :]
    go(nmt)
    half, wide = mids[0].ref.shape
    q = dot_tn(nmt[...], w()[...])
    qkv[...] = q.astype(BF16)
    go(qkv)
    row = jnp.sum(q * cot()[...].astype(F32), axis=1, keepdims=True)
    row = jnp.broadcast_to(row, (row.shape[0], 128)).T[:8, :]
    part[...] = row
    if msgs:
        if half < wide:
            row = jnp.concatenate([row, jnp.zeros((8, wide - half), F32)], axis=1)
        for k in range(n):
            msgs[k][:half, :] = mids[k]()[...]
            msgs[k][half:, :] = in_two(row)
            go(msgs[k])


def back_kernel(n, c, chans, m, ins, outs, go, evens, odds, whole, spare):
    seq_at = lax.axis_index("seq")
    core = lax.rem(lax.axis_index("dp"), 2)
    mids, parts = ins[:n], ins[n:-8]
    pooled, rtwo, conv_out, gmid, nin, gin, rone, taps = ins[-8:]
    send, keep, *msgs = outs
    half = rtwo().shape[0]
    r = rtwo()[...]
    atwo = pooled()[...] * r
    conv = conv_out()[...]
    sig = jax.nn.sigmoid(conv)
    slope = sig * (1.0 + conv * (1.0 - sig))
    gains = gmid()[pl.ds(seq_at, 1), :]
    mid, rowsum = 0.0, 0.0
    for v in mids:
        mid = mid + v()[:half, :].astype(F32)
    if parts:
        for v in parts:
            rowsum = rowsum + v()[...]
    else:
        for v in mids:
            rowsum = rowsum + joined(v()[half:, :])[:, :half]
    mean = jnp.concatenate([rowsum] * 16, axis=0).T[:, :1] * (1.0 / (2 * chans))
    section = r * (gains * mid - atwo * mean)
    cg = section * slope
    cg = cg.astype(BF16).astype(F32)
    ge, gd = cg[:, :c], cg[:, c:]
    bf = lambda v: v.astype(BF16)
    g0, gp, gm = bf(ge), bf(sooner(ge)), bf(later(ge))
    o0, op, om = bf(gd), bf(sooner(gd)), bf(later(gd))
    evens[...] = jnp.concatenate((gp, o0, g0, om, gm), axis=1)
    odds[...] = jnp.concatenate((op, gp, o0, g0, om), axis=1)
    wide, rows = chans // 2, 5 * c // (m // 2)
    nin = nin()
    for out, which in ((send, 1 - core), (keep, core)):
        at = pl.multiple_of(which * wide, wide & -wide)
        kg = dot_tn(evens[...], nin[:, pl.ds(at, wide)]) + dot_tn(odds[...], nin[:, pl.ds(chans + at, wide)])
        for q in range(m // 2):
            out[q] = kg[q * rows : (q + 1) * rows, :].astype(out.dtype)
        go(out)
    width = 2 * chans
    block = half // n
    gin, rone, taps = gin()[...], rone()[...], taps()[...]
    pick = picker((chans, c), seq_at, c)
    grad = section.astype(BF16)
    acc = 0.0
    lane = lax.broadcasted_iota(jnp.int32, (half, 128), 1)
    means = jnp.zeros((half, 128), F32)
    for h, g in ((0, evens), (1, odds)):
        ng = dot(g[...], taps)
        aone = nin[:, h * chans : (h + 1) * chans].astype(F32) / gin
        acc = acc + jnp.sum(ng * aone, axis=0, keepdims=True)
        placed = dot_nt(grad[:, h * c : (h + 1) * c], pick)
        means = jnp.where(lane == h, jnp.mean(placed * aone, axis=1, keepdims=True), means)
        total = (placed + rone[:, h : h + 1] * gin * ng).astype(BF16)
        whole[:, h * chans : (h + 1) * chans] = total
    spare[...] = means
    mid = jnp.sum(mid * atwo, axis=0, keepdims=True)
    short = -2 * c % 128
    if short:
        mid = jnp.concatenate([mid, jnp.zeros((1, short), F32)], axis=1)
    line = lax.broadcasted_iota(jnp.int32, (16, 128), 0)
    gains = jnp.zeros((16, 128), F32)
    vector = jnp.concatenate([acc, mid], axis=1)
    for i in range(vector.shape[1] // 128):
        gains = jnp.where(line == i, vector[:, i * 128 : (i + 1) * 128], gains)
    gains = in_two(gains)
    for k in range(n):
        at = pl.multiple_of(lax.rem(seq_at + k, n) * block, block)
        msgs[k][:, :width] = whole[pl.ds(at, block), :]
        msgs[k][:, width:] = jnp.zeros((block, 128), BF16)
        msgs[k][:32, width:] = gains
        mean = spare[pl.ds(at, block), :].T[:16, :]
        msgs[k][32:48, width : width + block] = mean.astype(BF16)
        go(msgs[k])


def weight_kernel(m, scale, ins, outs, go):
    core = lax.rem(lax.axis_index("dp"), 2)
    nms, total = ins[0](), 0.0
    for v, which in zip(ins[1:], (core, 1 - core)):
        v = v()
        for q in range(m // 2):
            total = total + dot(nms[2 * q + which], v[q])
    total = (total * scale).astype(BF16)
    for q in range(m // 2):
        outs[0][q] = total


def split_kernel(q, ins, outs, go):
    keep, recv = ins
    me = lax.axis_index("dp") // 2
    keep, recv = keep(), recv()
    for k in [*range(1, q), 0]:
        out = outs[k - 1]
        out[...] = (keep[me ^ k] + recv[me ^ k].astype(F32)).astype(out.dtype)


def finish_kernel(n, chans, scale, ins, outs, go):
    total = ins[0]()[...]
    for r in ins[1:-1]:
        total = total + r()[...].astype(F32)
    rows, wide = total.shape
    outs[0][:rows, :] = (total * scale).astype(BF16)
    gains = ins[-1]()
    pieces, count = wide // 128, chans // 128
    both = gains[0]
    for b in range(1, n):
        both = both + gains[b]
    line = lax.broadcasted_iota(jnp.int32, (8, wide), 0)
    tail = jnp.zeros((8, wide), F32)
    wanted = [(i, both, i * pieces) for i in range(2)] + [(2 + b, gains[b], count) for b in range(n)]
    for i, source, first in wanted:
        row = jnp.concatenate([source[first + j : first + j + 1, :] for j in range(pieces)], axis=1)
        tail = jnp.where(line == i, row, tail)
    outs[0][rows:, :] = in_two(tail * scale)


def half_kernel(q, ins, outs, go):
    me = lax.axis_index("dp") // 2
    out = outs[0]
    rows = ins[0].ref.shape[0] - 16
    tail = 0.0
    for k in range(q):
        at = pl.multiple_of((me ^ k) * rows, rows & -rows)
        out[pl.ds(at, rows), :] = ins[k]()[:rows, :]
        tail = tail + joined(ins[k]()[rows:, :])
    out[q * rows :, :] = in_two(tail)


def place_kernel(n, c, ins, outs, go):
    core = lax.rem(lax.axis_index("dp"), 2)
    mine, other = ins
    taps, gain_in, gain_mid = outs
    rows, wide = taps.shape[0], mine.ref.shape[1]
    total = 0.0
    for v, which in ((mine, core), (other, 1 - core)):
        side = pl.multiple_of(which * wide, wide & -wide)
        taps[:, pl.ds(side, wide)] = v()[:rows, :]
        total = total + joined(v()[rows:, :])
    gain_in[...] = jnp.concatenate([total[0:1, :], total[1:2, :]], axis=1).reshape(gain_in.shape)
    pieces = [total[2 + b : 3 + b, h * c : (h + 1) * c] for h in range(2) for b in range(n)]
    gain_mid[...] = jnp.concatenate(pieces, axis=1).reshape(gain_mid.shape)


def weave_kernel(mine, other, *refs):
    core = lax.rem(lax.axis_index("dp"), 2)
    out, sems = refs[-2:]
    copies = []
    for v, which in ((mine, core), (other, 1 - core)):
        for q in range(v.shape[0]):
            copies.append(pltpu.make_async_copy(v.at[q], out.at[q, which], sems.at[len(copies)]))
    for copy in copies:
        copy.start()
    for copy in copies:
        copy.wait()


def input_kernel(n, chans, ins, outs, go):
    me = lax.axis_index("seq")
    got, own = ins[:n], ins[n]
    out, gains = outs
    total = got[0]()[...].astype(F32)
    for v in got[1:]:
        total = total + v()[...].astype(F32)
    for k in range(n):
        gains[lax.rem(me - k + n, n)] = joined(got[k]()[:32, 2 * chans :])
    rows = total.shape[0]
    means = jnp.concatenate([total[32:48, 2 * chans :]] * 8, axis=0).T
    for h in range(2):
        x = own()[:, h * chans : (h + 1) * chans].astype(F32)
        a = x * inv_rms(x)
        t = total[:, h * chans : (h + 1) * chans]
        mean = means[:rows, h : h + 1]
        v = t - a * (jnp.mean(t * a, axis=-1, keepdims=True) - mean)
        out[:, h * chans : (h + 1) * chans] = v.astype(BF16)


def body(section_input, conv_kernel, qkv_weight, gain_in, gain_mid, qkv_cotangent):
    x = section_input[0]
    cot = qkv_cotangent[0]
    length, chans = x.shape
    c = conv_kernel.shape[2]
    width, cols = qkv_weight.shape
    n, m = lax.axis_size("seq"), lax.axis_size("dp")
    half = length // 2 * n
    scale = 1.0 / math.sqrt(m * half)
    shift = lambda v, k: lax.ppermute(v, "seq", [(i, (i + k) % n) for i in range(n)])
    from_all = lambda v: [v] + [shift(v, k) for k in range(1, n)]
    across = lambda v, k: lax.ppermute(v, "dp", [(i, i ^ k) for i in range(m)])
    same_core = [[i for i in range(m) if i % 2 == core] for core in range(2)]
    chips = m // 2
    rows, wide = 5 * c // chips, chans // 2

    taps_rows = conv_kernel.transpose(0, 2, 1).reshape(5 * c, chans)
    own = x.reshape(length // 2, width)
    xs = from_all(own)
    cots = jnp.broadcast_to(cot[None], (chips, *cot.shape))
    cots = lax.all_to_all(cots, "dp", 0, 0, axis_index_groups=same_core, tiled=True)
    used = [cot, qkv_weight, taps_rows]
    held = call(
        functools.partial(mid_kernel, n, c, chans),
        [gain_in, gain_mid],
        kept=[shaped((half, 2 * c), BF16)] * n + [shaped((1, chans), F32), shaped((n, 2 * c), F32)],
        fetch=used,
        flops=WAIT,
        name="mid_parts",
    )
    mid_msgs = held[:n]
    gin, gmid, cot, weight, taps = held[n:]
    pooled_msg, *states = call(
        functools.partial(conv_kernel_fwd, n, c, chans),
        [*xs, taps, gin],
        free=[shaped((half, 2 * c), BF16)],
        kept=[
            shaped((half, 2 * c), F32),
            shaped((half, 2 * c), F32),
            shaped((half, width), BF16),
            shaped((half, 2), F32),
        ],
        scratch=[pltpu.VMEM((half, width), BF16)],
        name="conv_forward",
    )
    blocks = from_all(pooled_msg)
    rides = half <= 2 * c
    nmt, rtwo, qkv, part, *tailed, pooled, conv_out, nin, rone = call(
        functools.partial(qkv_kernel, n, c, chans),
        [*blocks, *mid_msgs, gmid, cot, weight],
        outs=[
            shaped((width, half), BF16),
            shaped((half, 1), F32),
            shaped((half, cols), BF16),
            shaped((8, half), F32),
        ]
        + [shaped((half + 16, 2 * c), BF16)] * (n * rides),
        spill=states,
        name="qkv",
    )
    cots = gate(cots, nmt, pltpu.HBM)
    mid_msgs = tailed if rides else mid_msgs
    mids = [mid_msgs[0]] + [shift(mid_msgs[k], k) for k in range(1, n)]
    parts = [] if rides else from_all(part)
    nms = lax.all_to_all(nmt.reshape(m, width // m, half), "dp", 0, 0, tiled=True)
    (wshare,) = call(
        functools.partial(weight_kernel, m, scale),
        [nms, Far(cots), Far(across(cots, 1))],
        outs=[shaped((chips, width // m, cols), BF16)],
        name="weight_share",
    )
    whalf = lax.all_to_all(wshare, "dp", 0, 0, axis_index_groups=same_core, tiled=True)
    send, keep, *msgs = call(
        functools.partial(back_kernel, n, c, chans, m),
        [
            Far(mids[0]),
            *mids[1:],
            *parts,
            *map(Far, [pooled, rtwo, conv_out]),
            gmid,
            Far(nin),
            gin,
            Far(rone),
            Far(taps_rows),
        ],
        outs=[
            shaped((chips, rows, wide), BF16),
            shaped((chips, rows, wide), F32),
        ]
        + [shaped((half // n, width + 128), BF16)] * n,
        scratch=[
            pltpu.VMEM((half, 5 * c), BF16),
            pltpu.VMEM((half, 5 * c), BF16),
            pltpu.VMEM((half, width), BF16),
            pltpu.VMEM((half, 128), F32),
        ],
        after=[wshare],
        flops=WAIT,
        name="conv_backward",
    )
    got = [msgs[0]] + [shift(msgs[k], k) for k in range(1, n)]
    input_grad, gains = call(
        functools.partial(input_kernel, n, chans),
        [*got, own],
        free=[shaped((length // 2, width), BF16), shaped((n, 16, 128), F32)],
        name="input_grad",
    )
    *split, keep_sum = call(
        functools.partial(split_kernel, chips),
        [Far(keep), across(send, 1)],
        free=[shaped((rows, wide), BF16)] * (chips - 1),
        kept=[shaped((rows, wide), F32)],
        name="core_sum",
    )
    if rows % 16 == 0 and n <= 6:
        (kshare,) = call(
            functools.partial(finish_kernel, n, chans, scale),
            [keep_sum] + [across(split[k - 1], 2 * k) for k in range(1, chips)] + [gains],
            free=[shaped((rows + 16, wide), BF16)],
            name="chip_sum",
        )
        whalf = gate(whalf, kshare)
        within = lambda v: pltpu.with_memory_space_constraint(v, pltpu.VMEM)
        weight_grad = pl.pallas_call(
            weave_kernel,
            out_shape=pltpu.HBM((chips, 2, width // m, cols), BF16),
            in_specs=[VMEM, VMEM],
            out_specs=HBM,
            scratch_shapes=[pltpu.SemaphoreType.DMA((m,))],
            compiler_params=pltpu.CompilerParams(vmem_limit_bytes=SPARE << 20),
            cost_estimate=pl.CostEstimate(flops=0, bytes_accessed=0, transcendentals=0),
            name="weight_grad",
        )(within(whalf), within(across(whalf, 1)))
        kshares = [kshare] + [across(kshare, k) for k in range(2, m, 2)]
        (mine,) = call(
            functools.partial(half_kernel, chips),
            kshares,
            free=[shaped((5 * c + 16, wide), BF16)],
            after=[weight_grad],
            name="kernel_grad_half",
        )
        taps_grad, gain_in_grad, gain_mid_grad = call(
            functools.partial(place_kernel, n, c),
            [mine, across(mine, 1)],
            free=[shaped((5 * c, chans), BF16), shaped((chans,), F32), shaped((width,), F32)],
            name="kernel_grad",
        )
    else:
        core = lax.axis_index("dp") % 2
        both = jnp.stack([keep, send.astype(F32)])
        both = jnp.where(core == 0, both, both[::-1]).transpose(1, 2, 0, 3).reshape(5 * c, chans)
        both, gains = lax.psum((both, gains), "dp")
        taps_grad, gains = (both * scale).astype(BF16), gains * scale
        whalf = gate(whalf, gains)
        within = lambda v: pltpu.with_memory_space_constraint(v, pltpu.VMEM)
        weight_grad = pl.pallas_call(
            weave_kernel,
            out_shape=pltpu.HBM((chips, 2, width // m, cols), BF16),
            in_specs=[VMEM, VMEM],
            out_specs=HBM,
            scratch_shapes=[pltpu.SemaphoreType.DMA((m,))],
            compiler_params=pltpu.CompilerParams(vmem_limit_bytes=SPARE << 20),
            cost_estimate=pl.CostEstimate(flops=0, bytes_accessed=0, transcendentals=0),
            name="weight_grad",
        )(within(whalf), within(across(whalf, 1)))
        gain_in_grad = jnp.sum(gains[:, : chans // 128], axis=0)
        gain_mid_grad = gains[:, chans // 128 :].reshape(n, -1)[:, : 2 * c]
        gain_mid_grad = gain_mid_grad.reshape(n, 2, c).transpose(1, 0, 2)
    return (
        qkv[None],
        input_grad.reshape(1, length, chans),
        taps_grad.reshape(5, c, chans).transpose(0, 2, 1),
        gain_in_grad.reshape(chans),
        gain_mid_grad.reshape(width),
        weight_grad.reshape(width, cols),
    )


def solution(mesh):
    placed = (
        P("dp", "seq", None),
        P(None, None, "seq"),
        P(None, "seq"),
        P(),
        P(),
        P("dp", None, "seq"),
    )
    return jax.shard_map(
        body,
        mesh=mesh,
        in_specs=placed,
        out_specs=(
            P("dp", None, "seq"),
            P("dp", "seq", None),
            P(None, None, "seq"),
            P(),
            P(),
            P(None, "seq"),
        ),
        check_vma=False,
    )
```

```python
import functools
import math

import jax
import jax.numpy as jnp
from jax import lax
from jax.experimental import pallas as pl
from jax.experimental.pallas import tpu as pltpu
from jax.sharding import PartitionSpec as P

EPS = 1e-06
WAIT = 4e10
SPARE = 12
F32 = jnp.float32
BF16 = jnp.bfloat16
ANY = pl.BlockSpec(memory_space=pl.ANY)
HBM = pl.BlockSpec(memory_space=pltpu.HBM)
VMEM = pl.BlockSpec(memory_space=pltpu.VMEM)


class In:
    def __init__(self, ref, copy=None):
        self.ref, self.copy = ref, copy
        if copy is not None:
            copy.start()

    def __call__(self):
        if self.copy is not None:
            self.copy.wait()
            self.copy = None
        return self.ref


def shaped(shape, dtype):
    return jax.ShapeDtypeStruct(shape, dtype)


class Far:
    def __init__(self, value):
        self.value = value


def call(kernel, args, outs=(), free=(), kept=(), after=(), near=(), spill=(), fetch=(), scratch=(), flops=0, name=None):
    within = lambda v: pltpu.with_memory_space_constraint(v, pltpu.VMEM)
    near, spill = [within(v) for v in near], [within(v) for v in spill]
    fetch = [pltpu.with_memory_space_constraint(v, pltpu.HBM) for v in fetch]
    after = [pltpu.with_memory_space_constraint(v, pltpu.HBM) for v in after]
    far = [i for i, v in enumerate(args) if isinstance(v, Far)]
    args = [pltpu.with_memory_space_constraint(v.value, pltpu.HBM) if isinstance(v, Far) else v for v in args]
    count, skip = len(args), len(after) + len(near)
    lanes = lambda v: math.prod(v.shape[:-1]) * -(-v.shape[-1] // 128) * 128 * v.dtype.itemsize
    need = sum(map(lanes, [*args, *outs, *free, *scratch]))

    def whole(*refs):
        refs = list(refs)
        take = lambda k: [refs.pop(0) for _ in range(k)]
        ins, _, saved, fetched = take(count), take(skip), take(len(spill)), take(len(fetch))
        targets, rest, places, nears = take(len(outs)), take(len(free) + len(kept)), take(len(spill)), take(len(fetch))
        own, landed, made = take(len(scratch)), take(len(far)), take(len(outs))
        in_sems, out_sems = refs
        operands = [In(v) for v in ins]
        for k, i in enumerate(far):
            operands[i] = In(landed[k], pltpu.make_async_copy(ins[i], landed[k], in_sems.at[k]))
        pairs = [*zip(made, targets), *zip(saved, places), *zip(fetched, nears)]
        copies = [pltpu.make_async_copy(v, t, out_sems.at[k]) for k, (v, t) in enumerate(pairs)]
        operands += [In(t, copy) for t, copy in zip(nears, copies[len(pairs) - len(nears) :])]
        copies = copies[: len(pairs) - len(nears)]
        gone = [False] * len(made)

        def go(ref):
            k = next(i for i, v in enumerate(made) if v is ref)
            gone[k] = True
            copies[k].start()

        for copy in copies[len(made) :]:
            copy.start()
        kernel(operands, [*made, *rest], go, *own)
        for k, copy in enumerate(copies[: len(made)]):
            if not gone[k]:
                copy.start()
        for v in operands:
            v()
        for copy in copies:
            copy.wait()

    specs = [VMEM] * count
    for i in far:
        specs[i] = HBM
    memory = lambda space, values: [space(v.shape, v.dtype) for v in values]
    return pl.pallas_call(
        whole,
        out_shape=tuple(
            [*memory(pltpu.HBM, outs), *free, *memory(pltpu.VMEM, kept), *memory(pltpu.HBM, spill)]
            + memory(pltpu.VMEM, fetch)
        ),
        in_specs=specs + [HBM] * len(after) + [VMEM] * (len(near) + len(spill)) + [HBM] * len(fetch),
        out_specs=tuple([HBM] * len(outs) + [VMEM] * (len(free) + len(kept)) + [HBM] * len(spill) + [VMEM] * len(fetch)),
        scratch_shapes=[
            *scratch,
            *memory(pltpu.VMEM, [args[i] for i in far]),
            *memory(pltpu.VMEM, outs),
            pltpu.SemaphoreType.DMA((max(1, len(far)),)),
            pltpu.SemaphoreType.DMA((max(1, len(outs) + len(spill) + len(fetch)),)),
        ],
        compiler_params=pltpu.CompilerParams(vmem_limit_bytes=min(56 << 20, need + (SPARE << 20))),
        cost_estimate=pl.CostEstimate(flops=int(flops), bytes_accessed=0, transcendentals=0),
        name=name,
    )(*args, *after, *near, *spill, *fetch)


def gate(value, after, space=pltpu.VMEM):
    spec = pl.BlockSpec(memory_space=space)
    return pl.pallas_call(
        lambda *_: None,
        out_shape=space(value.shape, value.dtype),
        in_specs=[spec, ANY],
        out_specs=spec,
        input_output_aliases={0: 0},
        compiler_params=pltpu.CompilerParams(vmem_limit_bytes=SPARE << 20),
        cost_estimate=pl.CostEstimate(flops=0, bytes_accessed=0, transcendentals=0),
        name="gate",
    )(pltpu.with_memory_space_constraint(value, space), after)


def dot(a, b):
    return jnp.dot(a, b, preferred_element_type=F32)


def dot_nt(a, b):
    return lax.dot_general(a, b, (((1,), (1,)), ((), ())), preferred_element_type=F32)


def dot_tn(a, b):
    return lax.dot_general(a, b, (((0,), (0,)), ((), ())), preferred_element_type=F32)


def later(v):
    row = lax.broadcasted_iota(jnp.int32, v.shape, 0)
    return jnp.where(row == 0, 0.0, pltpu.roll(v, 1, 0))


def sooner(v):
    rows = v.shape[0]
    row = lax.broadcasted_iota(jnp.int32, v.shape, 0)
    return jnp.where(row == rows - 1, 0.0, pltpu.roll(v, rows - 1, 0))


def inv_rms(v):
    return lax.rsqrt(jnp.mean(v * v, axis=-1, keepdims=True) + EPS)


def in_two(v):
    high = v.astype(BF16).astype(F32)
    return jnp.concatenate([high, v - high], axis=0).astype(BF16)


def joined(tail):
    rows, tail = tail.shape[0] // 2, tail.astype(F32)
    return tail[:rows] + tail[rows:]


def picker(shape, me, c):
    row = lax.broadcasted_iota(jnp.int32, shape, 0)
    col = lax.broadcasted_iota(jnp.int32, shape, 1)
    return jnp.where(row == col + me * c, 1.0, 0.0).astype(BF16)


def mid_kernel(n, c, chans, ins, outs, go):
    me = lax.axis_index("seq")
    gain_in, gain_mid, cot, w = ins[:4]
    gin, gmid = outs[n:]
    gin[...] = gain_in()[...].reshape(1, chans)
    gains = gain_mid()[...].reshape(1, 2 * chans)
    for b in range(n):
        pair = [gains[:, h * chans + b * c : h * chans + (b + 1) * c] for h in range(2)]
        gmid[b : b + 1, :] = jnp.concatenate(pair, axis=1)
    g, w = cot()[...], w()
    for k in range(n):
        at = pl.multiple_of(lax.rem(me + k, n) * c, c & -c)
        rows = jnp.concatenate([w[pl.ds(at, c), :], w[pl.ds(chans + at, c), :]], axis=0)
        outs[k][...] = dot_nt(g, rows).astype(BF16)


def conv_kernel_fwd(n, c, chans, ins, outs, go, xs):
    me = lax.axis_index("seq")
    blocks, (taps, gain) = ins[:n], ins[n:]
    pooled_msg, pooled, conv_out, nin, rone = outs
    rows = blocks[0].ref.shape[0]
    gains = gain()[...]
    for k in range(n):
        at = pl.multiple_of(lax.rem(me - k + n, n) * rows, rows)
        v = blocks[k]()[...]
        xs[pl.ds(at, rows), :] = v
        for h in range(2):
            f = v[:, h * chans : (h + 1) * chans].astype(F32)
            r = inv_rms(f)
            rone[pl.ds(at, rows), h : h + 1] = r
            nin[pl.ds(at, rows), h * chans : (h + 1) * chans] = (f * r * gains).astype(BF16)
    nin = nin
    xe, xo = nin[:, :chans], nin[:, chans:]
    taps = taps()
    k0, k1, k2, k3, k4 = (taps[k * c : (k + 1) * c, :] for k in range(5))
    even = dot_nt(xe, k2) + dot_nt(xo, k3) + later(dot_nt(xe, k0) + dot_nt(xo, k1)) + sooner(dot_nt(xe, k4))
    odd = dot_nt(xe, k1) + dot_nt(xo, k2) + later(dot_nt(xo, k0)) + sooner(dot_nt(xe, k3) + dot_nt(xo, k4))
    conv = jnp.concatenate([even, odd], axis=1)
    pick = picker((chans, c), me, c)
    own = jnp.concatenate([dot(xs[:, :chans], pick), dot(xs[:, chans:], pick)], axis=1)
    total = own + conv * jax.nn.sigmoid(conv)
    pooled_msg[...] = total.astype(BF16)
    conv_out[...] = conv
    pooled[...] = total


def qkv_kernel(n, c, chans, ins, outs, go):
    me = lax.axis_index("seq")
    blocks, mids = ins[:n], ins[n : 2 * n]
    gains, cot, w = ins[2 * n :]
    nmt, rtwo, qkv, part, *msgs = outs
    squares = 0.0
    for v in blocks:
        v = v()[...].astype(F32)
        squares = squares + jnp.sum(v * v, axis=1, keepdims=True)
    r = lax.rsqrt(squares * (1.0 / (2 * chans)) + EPS)
    rtwo[...] = r
    gains = gains()
    for k in range(n):
        b = lax.rem(me - k + n, n)
        v = blocks[k]()[...].astype(F32) * r * gains[pl.ds(b, 1), :]
        t = v.T.astype(BF16)
        for h in range(2):
            at = pl.multiple_of(h * chans + b * c, c & -c)
            nmt[pl.ds(at, c), :] = t[h * c : (h + 1) * c, :]
    go(nmt)
    half, wide = mids[0].ref.shape
    q = dot_tn(nmt[...], w()[...])
    qkv[...] = q.astype(BF16)
    go(qkv)
    row = jnp.sum(q * cot()[...].astype(F32), axis=1, keepdims=True)
    row = jnp.broadcast_to(row, (row.shape[0], 128)).T[:8, :]
    part[...] = row
    if msgs:
        if half < wide:
            row = jnp.concatenate([row, jnp.zeros((8, wide - half), F32)], axis=1)
        for k in range(n):
            msgs[k][:half, :] = mids[k]()[...]
            msgs[k][half:, :] = in_two(row)
            go(msgs[k])


def back_kernel(n, c, chans, m, ins, outs, go, evens, odds, whole, spare):
    seq_at = lax.axis_index("seq")
    core = lax.rem(lax.axis_index("dp"), 2)
    mids, parts = ins[:n], ins[n:-8]
    pooled, rtwo, conv_out, gmid, nin, gin, rone, taps = ins[-8:]
    send, keep, *msgs = outs
    half = rtwo().shape[0]
    r = rtwo()[...]
    atwo = pooled()[...] * r
    conv = conv_out()[...]
    sig = jax.nn.sigmoid(conv)
    slope = sig * (1.0 + conv * (1.0 - sig))
    gains = gmid()[pl.ds(seq_at, 1), :]
    mid, rowsum = 0.0, 0.0
    for v in mids:
        mid = mid + v()[:half, :].astype(F32)
    if parts:
        for v in parts:
            rowsum = rowsum + v()[...]
    else:
        for v in mids:
            rowsum = rowsum + joined(v()[half:, :])[:, :half]
    mean = jnp.concatenate([rowsum] * 16, axis=0).T[:, :1] * (1.0 / (2 * chans))
    section = r * (gains * mid - atwo * mean)
    cg = section * slope
    cg = cg.astype(BF16).astype(F32)
    ge, gd = cg[:, :c], cg[:, c:]
    bf = lambda v: v.astype(BF16)
    g0, gp, gm = bf(ge), bf(sooner(ge)), bf(later(ge))
    o0, op, om = bf(gd), bf(sooner(gd)), bf(later(gd))
    evens[...] = jnp.concatenate((gp, o0, g0, om, gm), axis=1)
    odds[...] = jnp.concatenate((op, gp, o0, g0, om), axis=1)
    wide, rows = chans // 2, 5 * c // (m // 2)
    nin = nin()
    for out, which in ((send, 1 - core), (keep, core)):
        at = pl.multiple_of(which * wide, wide & -wide)
        kg = dot_tn(evens[...], nin[:, pl.ds(at, wide)]) + dot_tn(odds[...], nin[:, pl.ds(chans + at, wide)])
        for q in range(m // 2):
            out[q] = kg[q * rows : (q + 1) * rows, :].astype(out.dtype)
        go(out)
    width = 2 * chans
    block = half // n
    gin, rone, taps = gin()[...], rone()[...], taps()[...]
    pick = picker((chans, c), seq_at, c)
    grad = section.astype(BF16)
    acc = 0.0
    lane = lax.broadcasted_iota(jnp.int32, (half, 128), 1)
    means = jnp.zeros((half, 128), F32)
    for h, g in ((0, evens), (1, odds)):
        ng = dot(g[...], taps)
        aone = nin[:, h * chans : (h + 1) * chans].astype(F32) / gin
        acc = acc + jnp.sum(ng * aone, axis=0, keepdims=True)
        placed = dot_nt(grad[:, h * c : (h + 1) * c], pick)
        means = jnp.where(lane == h, jnp.mean(placed * aone, axis=1, keepdims=True), means)
        total = (placed + rone[:, h : h + 1] * gin * ng).astype(BF16)
        whole[:, h * chans : (h + 1) * chans] = total
    spare[...] = means
    mid = jnp.sum(mid * atwo, axis=0, keepdims=True)
    short = -2 * c % 128
    if short:
        mid = jnp.concatenate([mid, jnp.zeros((1, short), F32)], axis=1)
    line = lax.broadcasted_iota(jnp.int32, (16, 128), 0)
    gains = jnp.zeros((16, 128), F32)
    vector = jnp.concatenate([acc, mid], axis=1)
    for i in range(vector.shape[1] // 128):
        gains = jnp.where(line == i, vector[:, i * 128 : (i + 1) * 128], gains)
    gains = in_two(gains)
    for k in range(n):
        at = pl.multiple_of(lax.rem(seq_at + k, n) * block, block)
        msgs[k][:, :width] = whole[pl.ds(at, block), :]
        msgs[k][:, width:] = jnp.zeros((block, 128), BF16)
        msgs[k][:32, width:] = gains
        mean = spare[pl.ds(at, block), :].T[:16, :]
        msgs[k][32:48, width : width + block] = mean.astype(BF16)
        go(msgs[k])


def weight_kernel(m, scale, ins, outs, go):
    core = lax.rem(lax.axis_index("dp"), 2)
    nms, total = ins[0](), 0.0
    for v, which in zip(ins[1:], (core, 1 - core)):
        v = v()
        for q in range(m // 2):
            total = total + dot(nms[2 * q + which], v[q])
    total = (total * scale).astype(BF16)
    for q in range(m // 2):
        outs[0][q] = total


def split_kernel(q, ins, outs, go):
    keep, recv = ins
    me = lax.axis_index("dp") // 2
    keep, recv = keep(), recv()
    for k in [*range(1, q), 0]:
        out = outs[k - 1]
        out[...] = (keep[me ^ k] + recv[me ^ k].astype(F32)).astype(out.dtype)


def finish_kernel(n, chans, scale, ins, outs, go):
    total = ins[0]()[...]
    for r in ins[1:-1]:
        total = total + r()[...].astype(F32)
    rows, wide = total.shape
    outs[0][:rows, :] = (total * scale).astype(BF16)
    gains = ins[-1]()
    pieces, count = wide // 128, chans // 128
    both = gains[0]
    for b in range(1, n):
        both = both + gains[b]
    line = lax.broadcasted_iota(jnp.int32, (8, wide), 0)
    tail = jnp.zeros((8, wide), F32)
    wanted = [(i, both, i * pieces) for i in range(2)] + [(2 + b, gains[b], count) for b in range(n)]
    for i, source, first in wanted:
        row = jnp.concatenate([source[first + j : first + j + 1, :] for j in range(pieces)], axis=1)
        tail = jnp.where(line == i, row, tail)
    outs[0][rows:, :] = in_two(tail * scale)


def half_kernel(q, ins, outs, go):
    me = lax.axis_index("dp") // 2
    out = outs[0]
    rows = ins[0].ref.shape[0] - 16
    tail = 0.0
    for k in range(q):
        at = pl.multiple_of((me ^ k) * rows, rows & -rows)
        out[pl.ds(at, rows), :] = ins[k]()[:rows, :]
        tail = tail + joined(ins[k]()[rows:, :])
    out[q * rows :, :] = in_two(tail)


def place_kernel(n, c, ins, outs, go):
    core = lax.rem(lax.axis_index("dp"), 2)
    mine, other = ins
    taps, gain_in, gain_mid = outs
    rows, wide = taps.shape[0], mine.ref.shape[1]
    total = 0.0
    for v, which in ((mine, core), (other, 1 - core)):
        side = pl.multiple_of(which * wide, wide & -wide)
        taps[:, pl.ds(side, wide)] = v()[:rows, :]
        total = total + joined(v()[rows:, :])
    gain_in[...] = jnp.concatenate([total[0:1, :], total[1:2, :]], axis=1).reshape(gain_in.shape)
    pieces = [total[2 + b : 3 + b, h * c : (h + 1) * c] for h in range(2) for b in range(n)]
    gain_mid[...] = jnp.concatenate(pieces, axis=1).reshape(gain_mid.shape)


def weave_kernel(mine, other, *refs):
    core = lax.rem(lax.axis_index("dp"), 2)
    out, sems = refs[-2:]
    copies = []
    for v, which in ((mine, core), (other, 1 - core)):
        for q in range(v.shape[0]):
            copies.append(pltpu.make_async_copy(v.at[q], out.at[q, which], sems.at[len(copies)]))
    for copy in copies:
        copy.start()
    for copy in copies:
        copy.wait()


def input_kernel(n, chans, ins, outs, go):
    me = lax.axis_index("seq")
    got, own = ins[:n], ins[n]
    out, gains = outs
    total = got[0]()[...].astype(F32)
    for v in got[1:]:
        total = total + v()[...].astype(F32)
    for k in range(n):
        gains[lax.rem(me - k + n, n)] = joined(got[k]()[:32, 2 * chans :])
    rows = total.shape[0]
    means = jnp.concatenate([total[32:48, 2 * chans :]] * 8, axis=0).T
    for h in range(2):
        x = own()[:, h * chans : (h + 1) * chans].astype(F32)
        a = x * inv_rms(x)
        t = total[:, h * chans : (h + 1) * chans]
        mean = means[:rows, h : h + 1]
        v = t - a * (jnp.mean(t * a, axis=-1, keepdims=True) - mean)
        out[:, h * chans : (h + 1) * chans] = v.astype(BF16)


def body(section_input, conv_kernel, qkv_weight, gain_in, gain_mid, qkv_cotangent):
    x = section_input[0]
    cot = qkv_cotangent[0]
    length, chans = x.shape
    c = conv_kernel.shape[2]
    width, cols = qkv_weight.shape
    n, m = lax.axis_size("seq"), lax.axis_size("dp")
    half = length // 2 * n
    scale = 1.0 / math.sqrt(m * half)
    shift = lambda v, k: lax.ppermute(v, "seq", [(i, (i + k) % n) for i in range(n)])
    from_all = lambda v: [v] + [shift(v, k) for k in range(1, n)]
    across = lambda v, k: lax.ppermute(v, "dp", [(i, i ^ k) for i in range(m)])
    same_core = [[i for i in range(m) if i % 2 == core] for core in range(2)]
    chips = m // 2
    rows, wide = 5 * c // chips, chans // 2

    taps_rows = conv_kernel.transpose(0, 2, 1).reshape(5 * c, chans)
    own = x.reshape(length // 2, width)
    xs = from_all(own)
    cots = jnp.broadcast_to(cot[None], (chips, *cot.shape))
    cots = lax.all_to_all(cots, "dp", 0, 0, axis_index_groups=same_core, tiled=True)
    used = [cot, qkv_weight, taps_rows]
    held = call(
        functools.partial(mid_kernel, n, c, chans),
        [gain_in, gain_mid],
        kept=[shaped((half, 2 * c), BF16)] * n + [shaped((1, chans), F32), shaped((n, 2 * c), F32)],
        fetch=used,
        flops=WAIT,
        name="mid_parts",
    )
    mid_msgs = held[:n]
    gin, gmid, cot, weight, taps = held[n:]
    pooled_msg, *states = call(
        functools.partial(conv_kernel_fwd, n, c, chans),
        [*xs, taps, gin],
        free=[shaped((half, 2 * c), BF16)],
        kept=[
            shaped((half, 2 * c), F32),
            shaped((half, 2 * c), F32),
            shaped((half, width), BF16),
            shaped((half, 2), F32),
        ],
        scratch=[pltpu.VMEM((half, width), BF16)],
        name="conv_forward",
    )
    blocks = from_all(pooled_msg)
    rides = half <= 2 * c
    nmt, rtwo, qkv, part, *tailed, pooled, conv_out, nin, rone = call(
        functools.partial(qkv_kernel, n, c, chans),
        [*blocks, *mid_msgs, gmid, cot, weight],
        outs=[
            shaped((width, half), BF16),
            shaped((half, 1), F32),
            shaped((half, cols), BF16),
            shaped((8, half), F32),
        ]
        + [shaped((half + 16, 2 * c), BF16)] * (n * rides),
        spill=states,
        name="qkv",
    )
    cots = gate(cots, nmt, pltpu.HBM)
    mid_msgs = tailed if rides else mid_msgs
    mids = [mid_msgs[0]] + [shift(mid_msgs[k], k) for k in range(1, n)]
    parts = [] if rides else from_all(part)
    nms = lax.all_to_all(nmt.reshape(m, width // m, half), "dp", 0, 0, tiled=True)
    (wshare,) = call(
        functools.partial(weight_kernel, m, scale),
        [nms, Far(cots), Far(across(cots, 1))],
        outs=[shaped((chips, width // m, cols), BF16)],
        name="weight_share",
    )
    whalf = lax.all_to_all(wshare, "dp", 0, 0, axis_index_groups=same_core, tiled=True)
    send, keep, *msgs = call(
        functools.partial(back_kernel, n, c, chans, m),
        [
            Far(mids[0]),
            *mids[1:],
            *parts,
            *map(Far, [pooled, rtwo, conv_out]),
            gmid,
            Far(nin),
            gin,
            Far(rone),
            Far(taps_rows),
        ],
        outs=[
            shaped((chips, rows, wide), BF16),
            shaped((chips, rows, wide), F32),
        ]
        + [shaped((half // n, width + 128), BF16)] * n,
        scratch=[
            pltpu.VMEM((half, 5 * c), BF16),
            pltpu.VMEM((half, 5 * c), BF16),
            pltpu.VMEM((half, width), BF16),
            pltpu.VMEM((half, 128), F32),
        ],
        after=[wshare],
        flops=WAIT,
        name="conv_backward",
    )
    got = [msgs[0]] + [shift(msgs[k], k) for k in range(1, n)]
    input_grad, gains = call(
        functools.partial(input_kernel, n, chans),
        [*got, own],
        free=[shaped((length // 2, width), BF16), shaped((n, 16, 128), F32)],
        name="input_grad",
    )
    *split, keep_sum = call(
        functools.partial(split_kernel, chips),
        [keep, across(send, 1)],
        free=[shaped((rows, wide), BF16)] * (chips - 1),
        kept=[shaped((rows, wide), F32)],
        name="core_sum",
    )
    if rows % 16 == 0 and n <= 6:
        (kshare,) = call(
            functools.partial(finish_kernel, n, chans, scale),
            [keep_sum] + [across(split[k - 1], 2 * k) for k in range(1, chips)] + [gains],
            free=[shaped((rows + 16, wide), BF16)],
            name="chip_sum",
        )
        whalf = gate(whalf, kshare)
        within = lambda v: pltpu.with_memory_space_constraint(v, pltpu.VMEM)
        weight_grad = pl.pallas_call(
            weave_kernel,
            out_shape=pltpu.HBM((chips, 2, width // m, cols), BF16),
            in_specs=[VMEM, VMEM],
            out_specs=HBM,
            scratch_shapes=[pltpu.SemaphoreType.DMA((m,))],
            compiler_params=pltpu.CompilerParams(vmem_limit_bytes=SPARE << 20),
            cost_estimate=pl.CostEstimate(flops=0, bytes_accessed=0, transcendentals=0),
            name="weight_grad",
        )(within(whalf), within(across(whalf, 1)))
        kshares = [kshare] + [across(kshare, k) for k in range(2, m, 2)]
        (mine,) = call(
            functools.partial(half_kernel, chips),
            kshares,
            free=[shaped((5 * c + 16, wide), BF16)],
            after=[weight_grad],
            name="kernel_grad_half",
        )
        taps_grad, gain_in_grad, gain_mid_grad = call(
            functools.partial(place_kernel, n, c),
            [mine, across(mine, 1)],
            free=[shaped((5 * c, chans), BF16), shaped((chans,), F32), shaped((width,), F32)],
            name="kernel_grad",
        )
    else:
        core = lax.axis_index("dp") % 2
        both = jnp.stack([keep, send.astype(F32)])
        both = jnp.where(core == 0, both, both[::-1]).transpose(1, 2, 0, 3).reshape(5 * c, chans)
        both, gains = lax.psum((both, gains), "dp")
        taps_grad, gains = (both * scale).astype(BF16), gains * scale
        whalf = gate(whalf, gains)
        within = lambda v: pltpu.with_memory_space_constraint(v, pltpu.VMEM)
        weight_grad = pl.pallas_call(
            weave_kernel,
            out_shape=pltpu.HBM((chips, 2, width // m, cols), BF16),
            in_specs=[VMEM, VMEM],
            out_specs=HBM,
            scratch_shapes=[pltpu.SemaphoreType.DMA((m,))],
            compiler_params=pltpu.CompilerParams(vmem_limit_bytes=SPARE << 20),
            cost_estimate=pl.CostEstimate(flops=0, bytes_accessed=0, transcendentals=0),
            name="weight_grad",
        )(within(whalf), within(across(whalf, 1)))
        gain_in_grad = jnp.sum(gains[:, : chans // 128], axis=0)
        gain_mid_grad = gains[:, chans // 128 :].reshape(n, -1)[:, : 2 * c]
        gain_mid_grad = gain_mid_grad.reshape(n, 2, c).transpose(1, 0, 2)
    return (
        qkv[None],
        input_grad.reshape(1, length, chans),
        taps_grad.reshape(5, c, chans).transpose(0, 2, 1),
        gain_in_grad.reshape(chans),
        gain_mid_grad.reshape(width),
        weight_grad.reshape(width, cols),
    )


def solution(mesh):
    placed = (
        P("dp", "seq", None),
        P(None, None, "seq"),
        P(None, "seq"),
        P(),
        P(),
        P("dp", None, "seq"),
    )
    return jax.shard_map(
        body,
        mesh=mesh,
        in_specs=placed,
        out_specs=(
            P("dp", None, "seq"),
            P("dp", "seq", None),
            P(None, None, "seq"),
            P(),
            P(),
            P(None, "seq"),
        ),
        check_vma=False,
    )
```
